256 devices in a mesh: ctx: 32 (over y, x, core), exp: 8 (over z).
Axes of the slice: x: 4, y: 4, z: 8, core: 2. Of those that a mesh axis runs over, the one named last changes fastest.
Arguments:
- query: bfloat16 [3584, 6144], P('ctx', 'exp'), may hold values from -6 to 6
- keys: bfloat16 [3584, 6144], P('ctx', 'exp'), may hold values from -6 to 6
- values: bfloat16 [3584, 6144], P('ctx', 'exp'), may hold values from -6 to 6
- stream: bfloat16 [3584, 6144], P('ctx', 'exp'), may hold values from -6 to 6
- log_decay: float32 [3584, 48], P('ctx', 'exp'), may hold values from 0 to 1, as said below
- attn_gain: float32 [6144], P('exp'), may hold values from 0.1 to 1.9
- routes: int32 [3584, 2], P('ctx'), may hold values from 0 to 7, all different within a row; in each aligned block of 112 rows (0 to 111, 112 to 223, ...) at most 30 rows name the same one
- gate_weights: float32 [3584, 2], P('ctx'), may hold values from 0.2 to 1
- moe_gain: float32 [6144], replicated, may hold values from 0.1 to 1.9
- w_gate: bfloat16 [8, 6144, 9216], P('exp', None, 'ctx'), may hold values from -0.078125 to 0.078125
- w_up: bfloat16 [8, 6144, 9216], P('exp', None, 'ctx'), may hold values from -0.078125 to 0.078125
- w_down: bfloat16 [8, 9216, 6144], P('exp', 'ctx'), may hold values from -0.0625 to 0.0625
Outputs:
- mixed: bfloat16 [3584, 6144], P('ctx', 'exp')
The draws below stay inside these ranges and needn't reach their ends.
Inputs may be any that keep to these rules, and one draw needn't show every extreme that they name: The two experts of a position differ. In each aligned block of 112 positions no expert is named by more than 30 routes, and some expert reaches 30 in some block. `log_decay`: nonnegative decay rates, one for each head and position.
All inputs are finite; a program needn't handle non-finite values.
Results may differ from the reference program's by a relative error of at most 0.023.
Values may be sent and summed in bfloat16 or wider, within the bound.
No kernel may reach another device: no remote copies, remote signals or barrier semaphores. Data moves between devices by JAX's collectives and lax.ppermute only.
A program may use at most 128 MiB of HBM per device.

```python
import math
import jax
import jax.numpy as jnp
import numpy as np
from jax import lax

D = 6144
HEAD = 128
FF = 9216
HEADS = 48
SPAN = 112
EXPERTS = 8
CAP = 30
SEQ = 3584
N_CTX = 32


def draw_log_decay(key, part):
    key = jax.random.fold_in(key, 11)
    key_pick, key_fast, key_slow, key_rough, key_spots, key_sizes = jax.random.split(key, 6)
    share = 0.5
    fast = jax.random.bernoulli(key_pick, share, (HEADS,))
    fast_rate = jnp.exp(jax.random.uniform(key_fast, (HEADS,), minval=math.log(1.0 / 50.0), maxval=math.log(1.0 / 25.0)))
    slow_rate = jnp.exp(jax.random.uniform(key_slow, (HEADS,), minval=math.log(0.1), maxval=math.log(0.8))) / SEQ
    drawn_entries = jnp.where(fast, fast_rate, slow_rate)
    coarse_entries = jnp.exp(jax.random.uniform(key_rough, (SEQ, HEADS), minval=math.log(0.5), maxval=math.log(2.0)))
    spots = jax.random.randint(key_spots, (3,), 0, SEQ)
    cohort_lengths = jax.random.uniform(key_sizes, (3,), minval=0.22, maxval=0.45)
    specialist_tally = jnp.arange(SEQ, dtype=jnp.int32)[:, None] == spots[None, :]
    spike_entries = jnp.sum(jnp.where(specialist_tally, cohort_lengths[None, :], 0.0), axis=1)
    return (drawn_entries[None, :] * coarse_entries + spike_entries[:, None]).astype(jnp.float32)


def block_scale(own_key, dims, shards, least, largest):
    level = 1.0
    for dim, parts in shards:
        steps = jax.random.uniform(jax.random.fold_in(jax.random.fold_in(own_key, 6), dim), (parts,), jnp.float32, least / len(shards), largest / len(shards))
        level = level * jnp.repeat(jnp.exp(steps), dims[dim] // parts).reshape((-1,) + (1,) * (len(dims) - 1 - dim))
    return level


def shared_out(rng, own, number, rows, number_of, top, limit, skew):
    sequence = jax.random.permutation(rng, number_of)
    packed, common = load_shares(number_of, rows * top, limit, skew, True), load_shares(number_of, rows * top, limit, skew, False)
    places = jnp.arange(number_of)

    def named(sizes, turn):
        used = int((sizes > 0).sum())
        fixed = max(1, used // 4)
        passed = fixed + (places - fixed + turn * (used - fixed)) % max(1, number_of - fixed)
        return jnp.zeros((number_of,), jnp.int32).at[sequence[jnp.where(places < fixed, places, passed)]].set(jnp.asarray(sizes, jnp.int32))

    sizes = jnp.where(number % 4 == 0, named(packed, number // 4), named(common, number - number // 4 - 1))
    mixed = jax.random.permutation(jax.random.fold_in(own, 3), number_of)
    donor, receiver = mixed[0:number_of // 2 * 2:2], mixed[1:number_of // 2 * 2:2]
    room = jnp.minimum(sizes[donor] - 1, limit - sizes[receiver]) // 2
    room = jnp.where((donor == sequence[0]) | (receiver == sequence[0]) | (sizes[receiver] == 0), 0, jnp.maximum(room, 0))
    passed = jax.random.randint(jax.random.fold_in(own, 4), (number_of // 2,), 0, 1 << 20) % (room + 1)
    sizes = sizes.at[donor].add(-passed).at[receiver].add(passed)
    labels = jnp.searchsorted(jnp.cumsum(sizes), jnp.arange(rows * top), side="right").astype(jnp.int32)
    table = labels.reshape(top, rows).T
    table = table[jax.random.permutation(jax.random.fold_in(own, 1), rows)]
    turn = jax.random.randint(jax.random.fold_in(own, 2), (rows, 1), 0, top)
    return jnp.take_along_axis(table, (jnp.arange(top)[None, :] + turn) % top, axis=1)


def load_shares(amount, total, limit, lean, full):
    loads = [(1 << 20) // math.isqrt(rank ** lean) + 1 for rank in range(1, amount + 1)]
    largest = limit if full else min(limit, max(-(-total // amount), total * loads[0] // sum(loads)))
    least = 1 if total - largest >= amount - 1 else 0
    given, spare = [largest] + [least] * (amount - 1), total - largest - least * (amount - 1)
    while spare > 0:
        movable = [i for i in range(1, amount) if given[i] < largest] or [i for i in range(1, amount) if given[i] < limit]
        whole, remaining = sum([loads[i] for i in movable]), spare
        for i in movable:
            more = min(limit - given[i], max(1, remaining * loads[i] // whole), spare)
            given[i] = given[i] + more
            spare = spare - more
    return np.array(given)


def noise(own_key, dims, scale, bound, cuts=(), kind=jnp.bfloat16):
    level = block_scale(own_key, dims, cuts, -0.22, 0.18) if cuts else 1.0
    drawn = jax.random.normal(own_key, dims, jnp.float32) * scale * level
    return jnp.minimum(jnp.maximum(drawn, -bound), bound).astype(kind)


def setup_inputs(seed: int = 0) -> dict:
    seeds = jax.random.split(jax.random.key(seed), 13)
    query = noise(seeds[0], (SEQ, D), 1.0, 6.0, ((0, 32), (1, 8)))
    keys = noise(seeds[1], (SEQ, D), 1.0, 6.0, ((0, 32), (1, 8)))
    values = noise(seeds[2], (SEQ, D), 1.0, 6.0, ((0, 32), (1, 8)))
    stream = noise(seeds[3], (SEQ, D), 1.0, 6.0, ((0, 32), (1, 8)))
    log_decay = draw_log_decay(jax.random.fold_in(seeds[12], 71), 0)
    attn_gain = jnp.clip(1.0 + 0.18 * jax.random.normal(seeds[5], (D,), jnp.float32), 0.1, 1.9)
    routes_keys = jax.random.split(jax.random.fold_in(seeds[6], 1), SEQ // SPAN)
    routes_turns = jax.random.permutation(jax.random.fold_in(seeds[6], 3), SEQ // SPAN)
    routes = jax.vmap(lambda own, number: shared_out(jax.random.fold_in(seeds[6], 2), own, number, SPAN, EXPERTS, 2, CAP, 2))(routes_keys, routes_turns).reshape((SEQ, 2))
    gate_weights = jnp.clip(0.2 + 0.8 * jax.random.uniform(seeds[7], (SEQ, 2), jnp.float32) ** block_scale(seeds[7], (SEQ, 2), ((0, 32),), -0.2, 0.2), 0.2, 1.0)
    moe_gain = jnp.clip(1.0 + 0.18 * jax.random.normal(seeds[8], (D,), jnp.float32), 0.1, 1.9)
    w_gate = noise(seeds[9], (EXPERTS, D, FF), D ** -0.5, 0.078125, ((0, 8), (2, 32)))
    w_up = noise(seeds[10], (EXPERTS, D, FF), D ** -0.5, 0.078125, ((0, 8), (2, 32)))
    w_down = noise(seeds[11], (EXPERTS, FF, D), FF ** -0.5, 0.0625, ((0, 8), (1, 32)))
    return {"query": query, "keys": keys, "values": values, "stream": stream, "log_decay": log_decay, "attn_gain": attn_gain, "routes": routes, "gate_weights": gate_weights, "moe_gain": moe_gain, "w_gate": w_gate, "w_up": w_up, "w_down": w_down}


STABILIZER = 1e-05
HIGHEST = lax.Precision.HIGHEST

def route_slots(routes, capacity, experts):
    flat = routes.reshape(-1)
    onehot = (flat[:, None] == jnp.arange(experts, dtype=jnp.int32)[None, :]).astype(jnp.int32)
    before = jnp.cumsum(onehot, axis=0) - onehot
    within = lax.optimization_barrier(jnp.sum(before * onehot, axis=1)).astype(jnp.int32)
    return (flat * capacity + within).reshape(routes.shape).astype(jnp.int32)

def span_local(queries, keyed, valued, cumulated):
    length = cumulated.shape[0]
    positions = jnp.arange(length, dtype=jnp.int32)
    causal = (positions[:, None] >= positions[None, :])[:, None, :]
    spread = cumulated[:, :, None] - jnp.transpose(cumulated)[None, :, :]
    weights = jnp.where(causal, jnp.exp(-jnp.where(causal, spread, 0.0)), 0.0)
    scores = jnp.einsum('thd,shd->ths', queries, keyed, precision=HIGHEST)
    inside = jnp.einsum('ths,shd->thd', scores * weights, valued, precision=HIGHEST)
    tails = jnp.exp(cumulated - cumulated[-1][None, :])
    summary = jnp.einsum('sh,shd,she->hde', tails, keyed, valued, precision=HIGHEST)
    return (inside, summary, jnp.exp(-cumulated[-1]))

def normalize_heads(layer_results):
    return layer_results * lax.rsqrt(lax.optimization_barrier(jnp.mean(layer_results * layer_results, axis=-1, keepdims=True)) + STABILIZER)

def rms_rows(rows, gain):
    rows_f = rows.astype(jnp.float32)
    scale = lax.rsqrt(lax.optimization_barrier(jnp.mean(rows_f * rows_f, axis=-1, keepdims=True)) + STABILIZER)
    return (rows_f * scale * gain).astype(jnp.bfloat16)

def reference(query, keys, values, stream, log_decay, attn_gain, routes, gate_weights, moe_gain, w_gate, w_up, w_down):
    shape4 = (N_CTX, SPAN, HEADS, HEAD)
    queries = jax.nn.silu(query.astype(jnp.float32)).reshape(shape4)
    keyed = jax.nn.silu(keys.astype(jnp.float32)).reshape(shape4)
    valued = values.astype(jnp.float32).reshape(shape4)
    rates = log_decay.reshape(N_CTX, SPAN, HEADS)

    def advance(state, block):
        block_q, block_k, block_v, block_r = block
        cumulated = jnp.cumsum(block_r, axis=0)
        inside, summary, decay_total = span_local(block_q, block_k, block_v, cumulated)
        carried = jnp.einsum('th,thd,hde->the', jnp.exp(-cumulated), block_q, state, precision=HIGHEST)
        return (decay_total[:, None, None] * state + summary, inside + carried)
    start = jnp.zeros((HEADS, HEAD, HEAD), jnp.float32)
    _, attended = lax.scan(advance, start, (queries, keyed, valued, rates))
    normed = normalize_heads(attended).reshape(SEQ, D)
    hidden_state = (stream.astype(jnp.float32) + normed * attn_gain).astype(jnp.bfloat16)
    moe_input = rms_rows(hidden_state, moe_gain)
    slots = jax.vmap(lambda block: route_slots(block, CAP, EXPERTS))(routes.reshape(N_CTX, SPAN, 2))
    block_ids = jnp.broadcast_to(jnp.arange(N_CTX, dtype=jnp.int32)[:, None, None], (N_CTX, SPAN, 2))
    token_ids = jnp.broadcast_to(jnp.arange(SEQ, dtype=jnp.int32).reshape(N_CTX, SPAN)[:, :, None], (N_CTX, SPAN, 2))
    table = jnp.full((N_CTX, EXPERTS * CAP), -1, jnp.int32).at[block_ids, slots].set(token_ids)
    picked_rows = moe_input[jnp.maximum(table, 0)]
    gathered = jnp.where((table >= 0)[:, :, None], picked_rows, jnp.zeros((), jnp.bfloat16))
    gathered = gathered.reshape(N_CTX, EXPERTS, CAP, D).transpose(1, 0, 2, 3).reshape(EXPERTS, N_CTX * CAP, D)
    group = FF // N_CTX

    def expert(operands):
        rows, gate_matrix, up_matrix, down_matrix = operands
        gate_portion = jnp.dot(rows, gate_matrix, preferred_element_type=jnp.float32)
        up_part = jnp.dot(rows, up_matrix, preferred_element_type=jnp.float32)
        activated = (jax.nn.silu(gate_portion) * up_part).astype(jnp.bfloat16)
        split_hidden = activated.reshape(N_CTX * CAP, N_CTX, group).transpose(1, 0, 2)
        split_down = down_matrix.reshape(N_CTX, group, D)

        def accumulate(total, pieces):
            partial_sum = jnp.dot(pieces[0], pieces[1], preferred_element_type=jnp.float32).astype(jnp.bfloat16)
            partial_sum = lax.optimization_barrier(partial_sum)
            return (total + partial_sum.astype(jnp.float32), None)
        total, _ = lax.scan(accumulate, jnp.zeros((N_CTX * CAP, D), jnp.float32), (split_hidden, split_down))
        return total.astype(jnp.bfloat16)
    expert_out = lax.map(expert, (gathered, w_gate, w_up, w_down)).reshape(EXPERTS, N_CTX, CAP, D)
    chosen_experts = expert_out[slots // CAP, block_ids, slots % CAP].astype(jnp.float32)
    weights = gate_weights.reshape(N_CTX, SPAN, 2)
    moe = weights[:, :, 0, None] * chosen_experts[:, :, 0] + weights[:, :, 1, None] * chosen_experts[:, :, 1]
    mixed = hidden_state.astype(jnp.float32).reshape(N_CTX, SPAN, D) + moe
    return mixed.astype(jnp.bfloat16).reshape(SEQ, D)
```

```python
import jax
import jax.numpy as jnp
from jax import lax
from jax.experimental import pallas as pl
from jax.experimental.pallas import tpu as pltpu
from jax.sharding import PartitionSpec as P

STABILIZER = 1e-05
HIGHEST = lax.Precision.HIGHEST
F32 = jnp.float32
BF16 = jnp.bfloat16
NT = (((1,), (1,)), ((), ()))
TN = (((0,), (0,)), ((), ()))
SIDE = 4
CORES = 2
SLOTS = 32
GROUP = SIDE * SLOTS
PIECE = 24
FEATURES = 6144
HALF = FEATURES // 2
QUARTER = FEATURES // 4
STEP = 768


def whole(memory=pltpu.VMEM):
    return pl.BlockSpec(memory_space=memory)


def params(mib):
    return pltpu.CompilerParams(vmem_limit_bytes=mib << 20)


def shifted(dy, dx, flip=0):
    pairs = []
    for y in range(SIDE):
        for x in range(SIDE):
            for core in range(CORES):
                to = (y + dy) % SIDE * SIDE + (x + dx) % SIDE
                pairs.append(((y * SIDE + x) * CORES + core, to * CORES + (core + flip) % CORES))
    return pairs


def silu(v):
    return v / (1.0 + jnp.exp(-v))


def local_kernel(q_ref, k_ref, v_ref, rate_ref, piece_ref, inside_ref, decayed_ref, wide):
    length, width = q_ref.shape
    heads = rate_ref.shape[1]
    head = width // heads
    wide[...] = jnp.zeros_like(wide)
    wide[:, :heads] = rate_ref[...]
    rates = wide[...]
    row = lax.broadcasted_iota(jnp.int32, (length, length), 0)
    col = lax.broadcasted_iota(jnp.int32, (length, length), 1)
    causal = row >= col
    lower = causal.astype(F32)
    cumulated = jnp.dot(lower, rates, precision=HIGHEST, preferred_element_type=F32)
    across = lax.dot_general(
        rates, lower, (((0,), (1,)), ((), ())), precision=HIGHEST, preferred_element_type=F32
    )
    total = cumulated[length - 1 : length, :]
    states = []
    for h in range(heads):
        part = slice(h * head, (h + 1) * head)
        qa = silu(q_ref[:, part].astype(F32))
        ka = silu(k_ref[:, part].astype(F32))
        v = v_ref[:, part]
        down = cumulated[:, h : h + 1]
        spread = jnp.where(causal, down - across[h : h + 1, :], 0.0)
        weights = jnp.where(causal, jnp.exp(-spread), 0.0)
        scores = lax.dot_general(qa.astype(BF16), ka.astype(BF16), NT, preferred_element_type=F32)
        inside_ref[:, part] = jnp.dot(
            (scores * weights).astype(BF16), v, preferred_element_type=F32
        )
        tails = jnp.exp(down - total[:, h : h + 1])
        states.append(
            lax.dot_general((ka * tails).astype(BF16), v, TN, preferred_element_type=F32)
        )
        decayed_ref[:, part] = (qa * jnp.exp(-down)).astype(BF16)
    first = total.astype(BF16).astype(F32)
    second = (total - first).astype(BF16).astype(F32)
    third = total - first - second
    line = lax.broadcasted_iota(jnp.int32, (8, total.shape[1]), 0)
    notes = jnp.where(line == 0, first, jnp.where(line == 1, second, jnp.where(line == 2, third, 0.0)))
    count = piece_ref.shape[0]
    state = jnp.concatenate(states, axis=0).reshape(count, PIECE, head)
    notes = jnp.broadcast_to(notes[None], (count,) + notes.shape)
    piece_ref[...] = jnp.concatenate([state, notes], axis=1).astype(BF16)


def attend_locally(query, keys, values, log_decay, count):
    length, width = query.shape
    return pl.pallas_call(
        local_kernel,
        out_shape=(
            jax.ShapeDtypeStruct((count, PIECE + 8, 128), BF16),
            jax.ShapeDtypeStruct((length, width), F32),
            jax.ShapeDtypeStruct((length, width), BF16),
        ),
        in_specs=[whole()] * 4,
        out_specs=[whole()] * 3,
        scratch_shapes=[pltpu.VMEM((length, 128), F32)],
        compiler_params=params(24),
    )(query, keys, values, log_decay)


def scan_kernel(place_ref, pieces_ref, out_ref):
    count, rows, lanes = pieces_ref.shape
    pieces = pieces_ref[...].astype(F32)
    notes = pieces[:, PIECE:]
    total = notes[:, 0:1] + notes[:, 1:2] + notes[:, 2:3]
    row = lax.broadcasted_iota(jnp.int32, (PIECE, lanes), 0) + place_ref[0] * PIECE
    own = lax.shift_right_logical(row, 7) == lax.broadcasted_iota(jnp.int32, (PIECE, lanes), 1)
    decay = jnp.sum(jnp.where(own[None], jnp.exp(-total), 0.0), axis=-1, keepdims=True)
    state = jnp.zeros((PIECE, lanes), F32)
    blank = jnp.zeros((rows - PIECE, lanes), F32)
    for i in range(count):
        out_ref[i] = jnp.concatenate([state, blank], axis=0).astype(BF16)
        state = decay[i] * state + pieces[i, :PIECE]


def scan_states(place, pieces):
    return pl.pallas_call(
        scan_kernel,
        out_shape=jax.ShapeDtypeStruct(pieces.shape, BF16),
        in_specs=[whole(pltpu.SMEM), whole()],
        out_specs=whole(),
        compiler_params=params(16),
    )(place, pieces)


def hidden_kernel(
    state_ref, inside_ref, decayed_ref, stream_ref, gain_ref, routes_ref, hidden_ref, sent_ref, lead_ref, next_ref
):
    length, width = stream_ref.shape
    head = 128
    state = state_ref[...].astype(F32)[:, :PIECE].reshape(width, head).astype(BF16)
    for h in range(width // head):
        part = slice(h * head, (h + 1) * head)
        carried = jnp.dot(decayed_ref[:, part], state[part], preferred_element_type=F32)
        attended = inside_ref[:, part] + carried
        scale = lax.rsqrt(jnp.mean(attended * attended, axis=-1, keepdims=True) + STABILIZER)
        hidden_ref[:, part] = (
            stream_ref[:, part].astype(F32) + attended * scale * gain_ref[:, part]
        ).astype(BF16)
    lane = lax.broadcasted_iota(jnp.int32, (length, 128), 1)
    one = (lane == routes_ref[:, 0:1]).astype(F32)
    two = (lane == routes_ref[:, 1:2]).astype(F32)
    row = lax.broadcasted_iota(jnp.int32, (length, length), 0)
    col = lax.broadcasted_iota(jnp.int32, (length, length), 1)
    before = jnp.dot(
        (row > col).astype(BF16), (one + two).astype(BF16), preferred_element_type=F32
    )
    slot_one = jnp.sum(before * one, axis=-1, keepdims=True).astype(jnp.int32)
    slot_two = jnp.sum(before * two, axis=-1, keepdims=True).astype(jnp.int32)
    target = lax.broadcasted_iota(jnp.int32, lead_ref.shape, 1)
    lead = (target == routes_ref[:, 0:1] * SLOTS + slot_one).astype(F32).astype(BF16)
    follow = (target == routes_ref[:, 1:2] * SLOTS + slot_two).astype(F32).astype(BF16)
    lead_ref[...] = lead
    next_ref[...] = follow
    sent = lax.dot_general(lead + follow, hidden_ref[...], TN, preferred_element_type=F32)
    sent_ref[...] = sent.astype(BF16).reshape(sent_ref.shape)


def finish_attention(state, inside, decayed, stream, gain, routes, experts):
    length, width = stream.shape
    return pl.pallas_call(
        hidden_kernel,
        out_shape=(
            jax.ShapeDtypeStruct((length, width), BF16),
            jax.ShapeDtypeStruct((experts, SLOTS, width), BF16),
            jax.ShapeDtypeStruct((length, experts * SLOTS), BF16),
            jax.ShapeDtypeStruct((length, experts * SLOTS), BF16),
        ),
        in_specs=[whole()] * 6,
        out_specs=[whole()] * 4,
        compiler_params=params(16),
    )(state, inside, decayed, stream, gain, routes)


def norm_kernel(rows_ref, gain_ref, left_ref, right_ref):
    parts, _, width = rows_ref.shape
    rows = [rows_ref[i].astype(F32) for i in range(parts)]
    squares = sum(jnp.sum(r * r, axis=-1, keepdims=True) for r in rows)
    scale = lax.rsqrt(squares / (parts * width) + STABILIZER)
    for i, r in enumerate(rows):
        at = i * width
        ref = left_ref if at < HALF else right_ref
        value = (r * scale * gain_ref[:, at : at + width]).astype(BF16)
        ref[:, at % HALF : at % HALF + width] = value


def norm_rows(rows, gain):
    shape = jax.ShapeDtypeStruct((SLOTS, HALF), BF16)
    return pl.pallas_call(
        norm_kernel,
        out_shape=(shape, shape),
        in_specs=[whole()] * 2,
        out_specs=[whole()] * 2,
        compiler_params=params(16),
    )(rows, gain)


STEPS = FEATURES // STEP
PER_QUARTER = QUARTER // STEP


def up_kernel(groups, last, *refs):
    x_refs, refs = refs[: 4 * groups], refs[4 * groups :]
    weights, refs = refs[:4], refs[4:]
    if last:
        near_ref, side_ref, by_y_ref, by_x_ref, x_buf, sums = refs
    else:
        sums, x_buf = refs
    k = pl.program_id(0)
    for quarter in range(4):

        @pl.when(k // PER_QUARTER == quarter)
        def _():
            for g in range(groups):
                x_buf[g * GROUP : (g + 1) * GROUP] = x_refs[4 * g + quarter][...]

    half = k // (2 * PER_QUARTER)
    fresh = k % (2 * PER_QUARTER) == 0
    x = x_buf[...]
    for w, w_ref in enumerate(weights):
        product = jnp.dot(x, w_ref[...], preferred_element_type=F32)

        @pl.when(fresh)
        def _():
            sums[half, w] = product

        @pl.when(jnp.logical_not(fresh))
        def _():
            sums[half, w] += product

    if last:

        @pl.when(k == STEPS - 1)
        def _():
            def place(index, other):
                ref, start = ((near_ref, 0), (side_ref, 0), (side_ref, GROUP), (sums, 0))[index]
                return ref, slice(start + other * SLOTS, start + (other + 1) * SLOTS)

            for dy in range(SIDE):
                for dx in range(SIDE):
                    a_ref, a_rows = place(dy, dx)
                    b_ref, b_rows = place(dx, dy)
                    for pair in range(2):
                        gate = a_ref[0, 2 * pair, a_rows] + b_ref[1, 2 * pair, b_rows]
                        up = a_ref[0, 2 * pair + 1, a_rows] + b_ref[1, 2 * pair + 1, b_rows]
                        activated = (silu(gate) * up).astype(BF16)
                        at = dy * GROUP + dx * SLOTS
                        by_y_ref[pair, at : at + SLOTS] = activated
                        at = dx * GROUP + dy * SLOTS
                        by_x_ref[pair, at : at + SLOTS] = activated


def up_products(xs, weights, earlier=()):
    groups = len(xs) // 4
    hidden = weights[0].shape[1]
    rows = groups * GROUP

    def x_spec(quarter):
        first = quarter * PER_QUARTER
        return pl.BlockSpec(
            (GROUP, STEP), lambda k: (0, jnp.clip(k - first, 0, PER_QUARTER - 1))
        )

    sums = (2, 4, rows, hidden)
    in_specs = [x_spec(i % 4) for i in range(len(xs))]
    in_specs += [pl.BlockSpec((STEP, hidden), lambda k: (k, 0))] * 4
    in_specs += [whole()] * len(earlier)
    scratch = [pltpu.VMEM((rows, STEP), BF16)]
    if earlier:
        shape = jax.ShapeDtypeStruct((2, SIDE * GROUP, hidden), BF16)
        out_shape, out_specs = (shape, shape), [whole()] * 2
        scratch.append(pltpu.VMEM(sums, F32))
    else:
        out_shape, out_specs = jax.ShapeDtypeStruct(sums, F32), whole()
    return pl.pallas_call(
        lambda *refs: up_kernel(groups, bool(earlier), *refs),
        grid=(STEPS,),
        out_shape=out_shape,
        in_specs=in_specs,
        out_specs=out_specs,
        scratch_shapes=scratch,
        compiler_params=params(40),
        cost_estimate=pl.CostEstimate(
            flops=2 * rows * FEATURES * 4 * 512,
            bytes_accessed=FEATURES * 4 * 384 * 2,
            transcendentals=0,
        ),
    )(*xs, *weights, *earlier)


def down_kernel(act_ref, own_ref, other_ref, *out_refs):
    for i, ref in enumerate(out_refs):
        rows = slice(i * GROUP, (i + 1) * GROUP)
        total = jnp.dot(act_ref[0, rows], own_ref[...], preferred_element_type=F32)
        total += jnp.dot(act_ref[1, rows], other_ref[...], preferred_element_type=F32)
        ref[...] = total.astype(BF16)


def down_products(activated, own, other, quarter):
    hidden = own.shape[0]
    shape = jax.ShapeDtypeStruct((GROUP, QUARTER), BF16)
    spec = pl.BlockSpec((hidden, STEP), lambda n: (0, quarter * PER_QUARTER + n))
    return pl.pallas_call(
        down_kernel,
        grid=(PER_QUARTER,),
        out_shape=(shape,) * SIDE,
        in_specs=[whole(), spec, spec],
        out_specs=[pl.BlockSpec((GROUP, STEP), lambda n: (0, n))] * SIDE,
        compiler_params=params(24),
        cost_estimate=pl.CostEstimate(
            flops=2 * SIDE * GROUP * 1024 * QUARTER,
            bytes_accessed=2 * hidden * QUARTER * 2 + SIDE * GROUP * QUARTER * 2,
            transcendentals=0,
        ),
    )(activated, own, other)


def mix_kernel(back_ref, lead_ref, next_ref, gates_ref, hidden_ref, out_ref):
    rows = back_ref[...].reshape(lead_ref.shape[1], out_ref.shape[1])
    one = jnp.dot(lead_ref[...], rows, preferred_element_type=F32)
    two = jnp.dot(next_ref[...], rows, preferred_element_type=F32)
    gates = gates_ref[...]
    moe = gates[:, 0:1] * one + gates[:, 1:2] * two
    out_ref[...] = (hidden_ref[...].astype(F32) + moe).astype(BF16)


def mix(back, lead, follow, gates, hidden):
    return pl.pallas_call(
        mix_kernel,
        out_shape=jax.ShapeDtypeStruct(hidden.shape, BF16),
        in_specs=[whole()] * 5,
        out_specs=whole(),
        compiler_params=params(16),
    )(back, lead, follow, gates, hidden)


def send(x, dy, dx):
    return lax.ppermute(x, "ctx", shifted(dy, dx))


def turned(axis, distance):
    return (distance, 0) if axis == "y" else (0, distance)


def gather_first(block, axis):
    after = send(block, *turned(axis, -1))
    before = send(block, *turned(axis, 1))
    opposite = send(block, *turned(axis, 2))
    blocks = (block, after, before, opposite)
    return tuple(
        jnp.concatenate([b[:, i * QUARTER : (i + 1) * QUARTER] for b in blocks], axis=0)
        for i in range(2)
    )


def gather_second(own, axis):
    one, two = own
    after_one = send(one, *turned(axis, -1))
    before_two = send(two, *turned(axis, 1))
    after_two = send(two, *turned(axis, -1))
    before_one = send(one, *turned(axis, 1))
    opposite_one = send(after_one, *turned(axis, -1))
    opposite_two = send(before_two, *turned(axis, 1))
    return (after_one, after_two), (before_one, before_two), (opposite_one, opposite_two)


def added(*terms):
    return sum(t.astype(F32) for t in terms)


def scatter_first(one, two, axis):
    one_here, one_after, one_before, one_opposite = one
    two_here, two_after, two_before, two_opposite = two
    through_after = send(one_opposite, *turned(axis, 1))
    from_after_one = send(one_before, *turned(axis, -1))
    through_before = send(two_opposite, *turned(axis, -1))
    from_before_two = send(two_after, *turned(axis, 1))
    from_before_one = send(added(one_after, through_after).astype(BF16), *turned(axis, 1))
    from_after_two = send(added(two_before, through_before).astype(BF16), *turned(axis, -1))
    return (
        added(one_here, from_after_one, from_before_one),
        added(two_here, from_after_two, from_before_two),
    )


def scatter_second(sums, axis):
    blocks = jnp.concatenate(sums, axis=1).reshape(SIDE, SLOTS, HALF)
    rounded = blocks.astype(BF16)
    from_before = send(rounded[1], *turned(axis, 1))
    from_after = send(rounded[2], *turned(axis, -1))
    from_opposite = send(rounded[3], *turned(axis, 2))
    return added(blocks[0], from_before, from_after, from_opposite).astype(BF16)


def body(
    query,
    keys,
    values,
    stream,
    log_decay,
    attn_gain,
    routes,
    gate_weights,
    moe_gain,
    w_gate,
    w_up,
    w_down,
):
    experts = w_gate.shape[0] * lax.axis_size("exp")
    blocks = lax.axis_size("ctx")
    gate, up, down = w_gate[0], w_up[0], w_down[0]
    sibling = shifted(0, 0, 1)
    other_gate = lax.ppermute(gate, "ctx", sibling)
    other_up = lax.ppermute(up, "ctx", sibling)
    other_down = lax.ppermute(down, "ctx", sibling)

    pieces, inside, decayed = attend_locally(query, keys, values, log_decay, blocks)
    pieces = lax.all_to_all(pieces, "ctx", split_axis=0, concat_axis=0, tiled=True)
    place = lax.axis_index("ctx").astype(jnp.int32).reshape(1)
    states = scan_states(place, pieces)
    states = lax.all_to_all(states, "ctx", split_axis=0, concat_axis=0, tiled=True)
    hidden, sent, lead, follow = finish_attention(
        states, inside, decayed, stream, attn_gain.reshape(1, -1), routes, experts
    )
    arrived = lax.all_to_all(sent, "exp", split_axis=0, concat_axis=0, tiled=True)
    left, right = norm_rows(arrived, moe_gain.reshape(1, -1))

    left = gather_first(left, "x")
    right = gather_first(right, "y")
    left_after, left_before, left_opposite = gather_second(left, "y")
    right_after, right_before, right_opposite = gather_second(right, "x")
    weights = (gate, up, other_gate, other_up)
    near = up_products((*left, *right), weights)
    sides = up_products((*left_after, *right_after, *left_before, *right_before), weights)
    by_y, by_x = up_products((*left_opposite, *right_opposite), weights, (near, sides))

    left_one = down_products(by_y, down, other_down, 0)
    right_one = down_products(by_x, down, other_down, 2)
    left_two = down_products(by_y, down, other_down, 1)
    right_two = down_products(by_x, down, other_down, 3)
    left = scatter_second(scatter_first(left_one, left_two, "y"), "x")
    right = scatter_second(scatter_first(right_one, right_two, "x"), "y")
    summed = jnp.concatenate([left, right], axis=1)
    summed = jnp.transpose(summed.reshape(SLOTS, experts, -1), (1, 0, 2))
    returned = lax.all_to_all(summed, "exp", split_axis=0, concat_axis=0, tiled=True)
    return mix(returned, lead, follow, gate_weights, hidden)


def solution(mesh):
    return jax.shard_map(
        body,
        mesh=mesh,
        in_specs=(
            P("ctx", "exp"),
            P("ctx", "exp"),
            P("ctx", "exp"),
            P("ctx", "exp"),
            P("ctx", "exp"),
            P("exp"),
            P("ctx", None),
            P("ctx", None),
            P(),
            P("exp", None, "ctx"),
            P("exp", None, "ctx"),
            P("exp", "ctx", None),
        ),
        out_specs=P("ctx", "exp"),
        check_vma=False,
    )
```

```python
import jax
import jax.numpy as jnp
from jax import lax
from jax.experimental import pallas as pl
from jax.experimental.pallas import tpu as pltpu
from jax.sharding import PartitionSpec as P

STABILIZER = 1e-05
HIGHEST = lax.Precision.HIGHEST
F32 = jnp.float32
BF16 = jnp.bfloat16
NT = (((1,), (1,)), ((), ()))
TN = (((0,), (0,)), ((), ()))
SIDE = 4
CORES = 2
SLOTS = 32
GROUP = SIDE * SLOTS
PIECE = 24
FEATURES = 6144
HALF = FEATURES // 2


def whole(memory=pltpu.VMEM):
    return pl.BlockSpec(memory_space=memory)


def params(mib):
    return pltpu.CompilerParams(vmem_limit_bytes=mib << 20)


def chip_pairs(step, flip=0):
    pairs = []
    for y in range(SIDE):
        for x in range(SIDE):
            for core in range(CORES):
                dy, dx = step(core)
                to = (y + dy) % SIDE * SIDE + (x + dx) % SIDE
                pairs.append(((y * SIDE + x) * CORES + core, to * CORES + (core + flip) % CORES))
    return pairs


def send(rows, axis, distance):
    along_x = ((0, distance), (distance, 0))
    return lax.ppermute(rows, "ctx", chip_pairs(lambda core: along_x[(core + axis) % CORES]))


def silu(v):
    return v / (1.0 + jnp.exp(-v))


def local_kernel(q_ref, k_ref, v_ref, rate_ref, piece_ref, inside_ref, decayed_ref, wide):
    length, width = q_ref.shape
    heads = rate_ref.shape[1]
    head = width // heads
    wide[...] = jnp.zeros_like(wide)
    wide[:, :heads] = rate_ref[...]
    rates = wide[...]
    row = lax.broadcasted_iota(jnp.int32, (length, length), 0)
    col = lax.broadcasted_iota(jnp.int32, (length, length), 1)
    causal = row >= col
    lower = causal.astype(F32)
    cumulated = jnp.dot(lower, rates, precision=HIGHEST, preferred_element_type=F32)
    across = lax.dot_general(
        rates, lower, (((0,), (1,)), ((), ())), precision=HIGHEST, preferred_element_type=F32
    )
    total = cumulated[length - 1 : length, :]
    states = []
    for h in range(heads):
        part = slice(h * head, (h + 1) * head)
        qa = silu(q_ref[:, part].astype(F32))
        ka = silu(k_ref[:, part].astype(F32))
        v = v_ref[:, part]
        down = cumulated[:, h : h + 1]
        spread = jnp.where(causal, down - across[h : h + 1, :], 0.0)
        weights = jnp.where(causal, jnp.exp(-spread), 0.0)
        scores = lax.dot_general(qa.astype(BF16), ka.astype(BF16), NT, preferred_element_type=F32)
        inside_ref[:, part] = jnp.dot(
            (scores * weights).astype(BF16), v, preferred_element_type=F32
        )
        tails = jnp.exp(down - total[:, h : h + 1])
        states.append(
            lax.dot_general((ka * tails).astype(BF16), v, TN, preferred_element_type=F32)
        )
        decayed_ref[:, part] = (qa * jnp.exp(-down)).astype(BF16)
    first = total.astype(BF16).astype(F32)
    second = (total - first).astype(BF16).astype(F32)
    third = total - first - second
    line = lax.broadcasted_iota(jnp.int32, (8, total.shape[1]), 0)
    notes = jnp.where(line == 0, first, jnp.where(line == 1, second, jnp.where(line == 2, third, 0.0)))
    count = piece_ref.shape[0]
    state = jnp.concatenate(states, axis=0).reshape(count, PIECE, head)
    notes = jnp.broadcast_to(notes[None], (count,) + notes.shape)
    piece_ref[...] = jnp.concatenate([state, notes], axis=1).astype(BF16)


def attend_locally(query, keys, values, log_decay, count):
    length, width = query.shape
    return pl.pallas_call(
        local_kernel,
        out_shape=(
            jax.ShapeDtypeStruct((count, PIECE + 8, 128), BF16),
            jax.ShapeDtypeStruct((length, width), F32),
            jax.ShapeDtypeStruct((length, width), BF16),
        ),
        in_specs=[whole()] * 4,
        out_specs=[whole()] * 3,
        scratch_shapes=[pltpu.VMEM((length, 128), F32)],
        compiler_params=params(56),
    )(query, keys, values, log_decay)


def scan_kernel(place_ref, pieces_ref, out_ref):
    count, rows, lanes = pieces_ref.shape
    pieces = pieces_ref[...].astype(F32)
    notes = pieces[:, PIECE:]
    total = notes[:, 0:1] + notes[:, 1:2] + notes[:, 2:3]
    row = lax.broadcasted_iota(jnp.int32, (PIECE, lanes), 0) + place_ref[0] * PIECE
    own = lax.shift_right_logical(row, 7) == lax.broadcasted_iota(jnp.int32, (PIECE, lanes), 1)
    decay = jnp.sum(jnp.where(own[None], jnp.exp(-total), 0.0), axis=-1, keepdims=True)
    state = jnp.zeros((PIECE, lanes), F32)
    blank = jnp.zeros((rows - PIECE, lanes), F32)
    for i in range(count):
        out_ref[i] = jnp.concatenate([state, blank], axis=0).astype(BF16)
        state = decay[i] * state + pieces[i, :PIECE]


def scan_states(place, pieces):
    return pl.pallas_call(
        scan_kernel,
        out_shape=jax.ShapeDtypeStruct(pieces.shape, BF16),
        in_specs=[whole(pltpu.SMEM), whole()],
        out_specs=whole(),
        compiler_params=params(16),
    )(place, pieces)


def hidden_kernel(
    state_ref, inside_ref, decayed_ref, stream_ref, gain_ref, routes_ref, hidden_ref, sent_ref, lead_ref, next_ref
):
    length, width = stream_ref.shape
    head = 128
    state = state_ref[...].astype(F32)[:, :PIECE].reshape(width, head).astype(BF16)
    for h in range(width // head):
        part = slice(h * head, (h + 1) * head)
        carried = jnp.dot(decayed_ref[:, part], state[part], preferred_element_type=F32)
        attended = inside_ref[:, part] + carried
        scale = lax.rsqrt(jnp.mean(attended * attended, axis=-1, keepdims=True) + STABILIZER)
        hidden_ref[:, part] = (
            stream_ref[:, part].astype(F32) + attended * scale * gain_ref[:, part]
        ).astype(BF16)
    lane = lax.broadcasted_iota(jnp.int32, (length, 128), 1)
    one = (lane == routes_ref[:, 0:1]).astype(F32)
    two = (lane == routes_ref[:, 1:2]).astype(F32)
    row = lax.broadcasted_iota(jnp.int32, (length, length), 0)
    col = lax.broadcasted_iota(jnp.int32, (length, length), 1)
    before = jnp.dot(
        (row > col).astype(BF16), (one + two).astype(BF16), preferred_element_type=F32
    )
    slot_one = jnp.sum(before * one, axis=-1, keepdims=True).astype(jnp.int32)
    slot_two = jnp.sum(before * two, axis=-1, keepdims=True).astype(jnp.int32)
    target = lax.broadcasted_iota(jnp.int32, lead_ref.shape, 1)
    lead = (target == routes_ref[:, 0:1] * SLOTS + slot_one).astype(F32).astype(BF16)
    follow = (target == routes_ref[:, 1:2] * SLOTS + slot_two).astype(F32).astype(BF16)
    lead_ref[...] = lead
    next_ref[...] = follow
    sent = lax.dot_general(lead + follow, hidden_ref[...], TN, preferred_element_type=F32)
    sent_ref[...] = sent.astype(BF16).reshape(sent_ref.shape)


def finish_attention(state, inside, decayed, stream, gain, routes, experts):
    length, width = stream.shape
    return pl.pallas_call(
        hidden_kernel,
        out_shape=(
            jax.ShapeDtypeStruct((length, width), BF16),
            jax.ShapeDtypeStruct((experts, SLOTS, width), BF16),
            jax.ShapeDtypeStruct((length, experts * SLOTS), BF16),
            jax.ShapeDtypeStruct((length, experts * SLOTS), BF16),
        ),
        in_specs=[whole()] * 6,
        out_specs=[whole()] * 4,
        compiler_params=params(56),
    )(state, inside, decayed, stream, gain, routes)


def norm_kernel(rows_ref, gain_ref, out_ref):
    parts, _, width = rows_ref.shape
    rows = [rows_ref[i].astype(F32) for i in range(parts)]
    squares = sum(jnp.sum(r * r, axis=-1, keepdims=True) for r in rows)
    scale = lax.rsqrt(squares / (parts * width) + STABILIZER)
    for i, r in enumerate(rows):
        part = slice(i * width, (i + 1) * width)
        out_ref[:, part] = (r * scale * gain_ref[:, part]).astype(BF16)


def norm_rows(rows, gain):
    return pl.pallas_call(
        norm_kernel,
        out_shape=jax.ShapeDtypeStruct((SLOTS, FEATURES), BF16),
        in_specs=[whole()] * 2,
        out_specs=whole(),
        compiler_params=params(16),
    )(rows, gain)


PACKED = 640
CHUNK = 1536
LIMIT = 18


def expert_kernel(groups, *refs):
    x_refs, refs = refs[:groups], refs[groups:]
    up_refs, down_refs, refs = refs[:4], refs[4:6], refs[6:]
    out_refs, sums = refs[:-1], refs[-1]
    hidden = up_refs[0].shape[0]
    width = x_refs[0].shape[1]
    for at in range(0, width, CHUNK):
        part = slice(at, at + CHUNK)
        x = jnp.concatenate([ref[:, part] for ref in x_refs], axis=0)
        for w, ref in enumerate(up_refs):
            product = lax.dot_general(ref[:, part], x, NT, preferred_element_type=F32)
            sums[w] = product if at == 0 else sums[w] + product

    rows = groups * GROUP
    blank = PACKED - 2 * hidden
    activated = [silu(sums[2 * w]) * sums[2 * w + 1] for w in range(2)]
    activated.append(jnp.zeros((blank, rows), F32))
    activated = jnp.transpose(jnp.concatenate(activated, axis=0)).astype(BF16)

    for at in range(0, FEATURES, CHUNK):
        half, start = divmod(at, HALF)
        weights = [ref[:, at : at + CHUNK] for ref in down_refs]
        weights = jnp.concatenate(weights + [jnp.zeros((blank, CHUNK), BF16)], axis=0)
        product = jnp.dot(activated, weights, preferred_element_type=F32).astype(BF16)
        for g in range(groups):
            out_refs[2 * g + half][:, start : start + CHUNK] = product[g * GROUP : (g + 1) * GROUP]


def expert(xs, ups, downs):
    groups = len(xs)
    hidden = ups[0].shape[0]
    rows = groups * GROUP
    return pl.pallas_call(
        lambda *refs: expert_kernel(groups, *refs),
        out_shape=(jax.ShapeDtypeStruct((GROUP, HALF), BF16),) * (2 * groups),
        in_specs=[whole()] * (groups + 6),
        out_specs=(whole(),) * (2 * groups),
        scratch_shapes=[pltpu.VMEM((4, hidden, rows), F32)],
        compiler_params=params(LIMIT),
        cost_estimate=pl.CostEstimate(
            flops=2 * 256 * FEATURES * 6 * hidden,
            bytes_accessed=FEATURES * 6 * hidden * 2,
            transcendentals=0,
        ),
    )(*xs, *ups, *downs)


def mix_kernel(back_ref, lead_ref, next_ref, gates_ref, hidden_ref, out_ref):
    rows = back_ref[...].reshape(lead_ref.shape[1], out_ref.shape[1])
    one = jnp.dot(lead_ref[...], rows, preferred_element_type=F32)
    two = jnp.dot(next_ref[...], rows, preferred_element_type=F32)
    gates = gates_ref[...]
    moe = gates[:, 0:1] * one + gates[:, 1:2] * two
    out_ref[...] = (hidden_ref[...].astype(F32) + moe).astype(BF16)


def mix(back, lead, follow, gates, hidden):
    return pl.pallas_call(
        mix_kernel,
        out_shape=jax.ShapeDtypeStruct(hidden.shape, BF16),
        in_specs=[whole()] * 5,
        out_specs=whole(),
        compiler_params=params(16),
    )(back, lead, follow, gates, hidden)


FIRST, SECOND = 0, 1


def gather_first(block):
    after = send(block, FIRST, -1)
    before = send(block, FIRST, 1)
    opposite = send(block, FIRST, 2)
    blocks = (block, after, before, opposite)
    return jnp.concatenate(blocks, axis=0)


def added(*terms):
    return sum(t.astype(F32) for t in terms)


def body(
    query,
    keys,
    values,
    stream,
    log_decay,
    attn_gain,
    routes,
    gate_weights,
    moe_gain,
    w_gate,
    w_up,
    w_down,
):
    experts = w_gate.shape[0] * lax.axis_size("exp")
    blocks = lax.axis_size("ctx")
    gate, up, down = w_gate[0].T, w_up[0].T, w_down[0]
    sibling = chip_pairs(lambda core: (0, 0), 1)
    other_gate = lax.ppermute(gate, "ctx", sibling)
    other_up = lax.ppermute(up, "ctx", sibling)
    other_down = lax.ppermute(down, "ctx", sibling)

    pieces, inside, decayed = attend_locally(query, keys, values, log_decay, blocks)
    pieces = lax.all_to_all(pieces, "ctx", split_axis=0, concat_axis=0, tiled=True)
    place = lax.axis_index("ctx").astype(jnp.int32).reshape(1)
    states = scan_states(place, pieces)
    states = lax.all_to_all(states, "ctx", split_axis=0, concat_axis=0, tiled=True)
    states, other_gate, other_up, other_down = lax.optimization_barrier(
        (states, other_gate, other_up, other_down)
    )
    hidden, sent, lead, follow = finish_attention(
        states, inside, decayed, stream, attn_gain.reshape(1, -1), routes, experts
    )
    arrived = lax.all_to_all(sent, "exp", split_axis=0, concat_axis=0, tiled=True)
    rows = norm_rows(arrived, moe_gain.reshape(1, -1))
    ups, downs = (gate, up, other_gate, other_up), (down, other_down)

    own = gather_first(rows)
    after = send(own, SECOND, -1)
    before = send(own, SECOND, 1)
    here_one, here_two = expert((own,), ups, downs)
    after, before, here_one, here_two = lax.optimization_barrier(
        (after, before, here_one, here_two)
    )
    opposite_one = send(after[:, :HALF], SECOND, -1)
    opposite_two = send(before[:, HALF:], SECOND, 1)
    to_after_one, to_after_two, to_before_one, to_before_two = expert((after, before), ups, downs)
    from_after_one = send(to_before_one, SECOND, -1)
    from_before_two = send(to_after_two, SECOND, 1)
    opposite = jnp.concatenate([opposite_one, opposite_two], axis=1)
    opposite, to_after_one, to_after_two, to_before_one, to_before_two = lax.optimization_barrier(
        (opposite, to_after_one, to_after_two, to_before_one, to_before_two)
    )
    far_one, far_two = expert((opposite,), ups, downs)
    far_one, far_two, from_after_one, from_before_two = lax.optimization_barrier(
        (far_one, far_two, from_after_one, from_before_two)
    )
    through_after = send(far_one, SECOND, 1)
    through_before = send(far_two, SECOND, -1)
    from_before_one = send(added(to_after_one, through_after).astype(BF16), SECOND, 1)
    from_after_two = send(added(to_before_two, through_before).astype(BF16), SECOND, -1)
    sums = jnp.concatenate(
        [
            added(here_one, from_after_one, from_before_one),
            added(here_two, from_after_two, from_before_two),
        ],
        axis=1,
    ).reshape(SIDE, SLOTS, FEATURES)
    rounded = sums.astype(BF16)
    from_before = send(rounded[1], FIRST, 1)
    from_after = send(rounded[2], FIRST, -1)
    from_opposite = send(rounded[3], FIRST, 2)
    summed = added(sums[0], from_before, from_after, from_opposite).astype(BF16)
    summed = jnp.transpose(summed.reshape(SLOTS, experts, -1), (1, 0, 2))
    returned = lax.all_to_all(summed, "exp", split_axis=0, concat_axis=0, tiled=True)
    return mix(returned, lead, follow, gate_weights, hidden)


def solution(mesh):
    return jax.shard_map(
        body,
        mesh=mesh,
        in_specs=(
            P("ctx", "exp"),
            P("ctx", "exp"),
            P("ctx", "exp"),
            P("ctx", "exp"),
            P("ctx", "exp"),
            P("exp"),
            P("ctx", None),
            P("ctx", None),
            P(),
            P("exp", None, "ctx"),
            P("exp", None, "ctx"),
            P("exp", "ctx", None),
        ),
        out_specs=P("ctx", "exp"),
        check_vma=False,
    )
```

```python
import jax
import jax.numpy as jnp
from jax import lax
from jax.experimental import pallas as pl
from jax.experimental.pallas import tpu as pltpu
from jax.sharding import PartitionSpec as P

STABILIZER = 1e-05
HIGHEST = lax.Precision.HIGHEST
F32 = jnp.float32
BF16 = jnp.bfloat16
NT = (((1,), (1,)), ((), ()))
TN = (((0,), (0,)), ((), ()))
SIDE = 4
CORES = 2
SLOTS = 32
GROUP = SIDE * SLOTS
PIECE = 24
FEATURES = 6144
HALF = FEATURES // 2


def whole(memory=pltpu.VMEM):
    return pl.BlockSpec(memory_space=memory)


def params(mib):
    return pltpu.CompilerParams(vmem_limit_bytes=mib << 20)


def chip_pairs(step, flip=0):
    pairs = []
    for y in range(SIDE):
        for x in range(SIDE):
            for core in range(CORES):
                dy, dx = step(core)
                to = (y + dy) % SIDE * SIDE + (x + dx) % SIDE
                pairs.append(((y * SIDE + x) * CORES + core, to * CORES + (core + flip) % CORES))
    return pairs


def send(rows, axis, distance):
    along_x = ((0, distance), (distance, 0))
    return lax.ppermute(rows, "ctx", chip_pairs(lambda core: along_x[(core + axis) % CORES]))


def silu(v):
    return v / (1.0 + jnp.exp(-v))


def local_kernel(q_ref, k_ref, v_ref, rate_ref, piece_ref, inside_ref, decayed_ref, wide):
    length, width = q_ref.shape
    heads = rate_ref.shape[0]
    head = width // heads
    wide[...] = jnp.zeros_like(wide)
    wide[:heads] = rate_ref[...]
    rates = wide[...]
    row = lax.broadcasted_iota(jnp.int32, (length, length), 0)
    col = lax.broadcasted_iota(jnp.int32, (length, length), 1)
    causal = row >= col
    lower = causal.astype(F32)
    cumulated = lax.dot_general(lower, rates, NT, precision=HIGHEST, preferred_element_type=F32)
    across = lax.dot_general(
        rates[:8], lower, NT, precision=HIGHEST, preferred_element_type=F32
    )
    total = cumulated[length - 1 : length, :]
    states = []
    for h in range(heads):
        part = slice(h * head, (h + 1) * head)
        qa = silu(q_ref[:, part].astype(F32))
        ka = silu(k_ref[:, part].astype(F32))
        v = v_ref[:, part]
        down = cumulated[:, h : h + 1]
        spread = jnp.where(causal, down - across[h : h + 1, :], 0.0)
        weights = jnp.where(causal, jnp.exp(-spread), 0.0)
        scores = lax.dot_general(qa.astype(BF16), ka.astype(BF16), NT, preferred_element_type=F32)
        inside_ref[:, part] = jnp.dot(
            (scores * weights).astype(BF16), v, preferred_element_type=F32
        )
        tails = jnp.exp(down - total[:, h : h + 1])
        states.append(
            lax.dot_general((ka * tails).astype(BF16), v, TN, preferred_element_type=F32)
        )
        decayed_ref[:, part] = (qa * jnp.exp(-down)).astype(BF16)
    first = total.astype(BF16).astype(F32)
    second = (total - first).astype(BF16).astype(F32)
    third = total - first - second
    line = lax.broadcasted_iota(jnp.int32, (8, total.shape[1]), 0)
    notes = jnp.where(line == 0, first, jnp.where(line == 1, second, jnp.where(line == 2, third, 0.0)))
    count = piece_ref.shape[0]
    state = jnp.concatenate(states, axis=0).reshape(count, PIECE, head)
    notes = jnp.broadcast_to(notes[None], (count,) + notes.shape)
    piece_ref[...] = jnp.concatenate([state, notes], axis=1).astype(BF16)


def attend_locally(query, keys, values, log_decay, count):
    length, width = query.shape
    return pl.pallas_call(
        local_kernel,
        out_shape=(
            jax.ShapeDtypeStruct((count, PIECE + 8, 128), BF16),
            jax.ShapeDtypeStruct((length, width), F32),
            jax.ShapeDtypeStruct((length, width), BF16),
        ),
        in_specs=[whole()] * 4,
        out_specs=[whole()] * 3,
        scratch_shapes=[pltpu.VMEM((128, length), F32)],
        compiler_params=params(56),
    )(query, keys, values, log_decay)


def scan_kernel(place_ref, pieces_ref, out_ref):
    count, rows, lanes = pieces_ref.shape
    pieces = pieces_ref[...].astype(F32)
    notes = pieces[:, PIECE:]
    total = notes[:, 0:1] + notes[:, 1:2] + notes[:, 2:3]
    row = lax.broadcasted_iota(jnp.int32, (PIECE, lanes), 0) + place_ref[0] * PIECE
    own = lax.shift_right_logical(row, 7) == lax.broadcasted_iota(jnp.int32, (PIECE, lanes), 1)
    decay = jnp.sum(jnp.where(own[None], jnp.exp(-total), 0.0), axis=-1, keepdims=True)
    state = jnp.zeros((PIECE, lanes), F32)
    blank = jnp.zeros((rows - PIECE, lanes), F32)
    for i in range(count):
        out_ref[i] = jnp.concatenate([state, blank], axis=0).astype(BF16)
        state = decay[i] * state + pieces[i, :PIECE]


def scan_states(place, pieces):
    return pl.pallas_call(
        scan_kernel,
        out_shape=jax.ShapeDtypeStruct(pieces.shape, BF16),
        in_specs=[whole(pltpu.SMEM), whole()],
        out_specs=whole(),
        compiler_params=params(16),
    )(place, pieces)


def hidden_kernel(
    state_ref, inside_ref, decayed_ref, stream_ref, gain_ref, routes_ref, hidden_ref, sent_ref, lead_ref, next_ref
):
    length, width = stream_ref.shape
    head = 128
    state = state_ref[...].astype(F32)[:, :PIECE].reshape(width, head).astype(BF16)
    for h in range(width // head):
        part = slice(h * head, (h + 1) * head)
        carried = jnp.dot(decayed_ref[:, part], state[part], preferred_element_type=F32)
        attended = inside_ref[:, part] + carried
        scale = lax.rsqrt(jnp.mean(attended * attended, axis=-1, keepdims=True) + STABILIZER)
        hidden_ref[:, part] = (
            stream_ref[:, part].astype(F32) + attended * scale * gain_ref[:, part]
        ).astype(BF16)
    lane = lax.broadcasted_iota(jnp.int32, (length, 128), 1)
    one = (lane == routes_ref[:, 0:1]).astype(F32)
    two = (lane == routes_ref[:, 1:2]).astype(F32)
    row = lax.broadcasted_iota(jnp.int32, (length, length), 0)
    col = lax.broadcasted_iota(jnp.int32, (length, length), 1)
    before = jnp.dot(
        (row > col).astype(BF16), (one + two).astype(BF16), preferred_element_type=F32
    )
    slot_one = jnp.sum(before * one, axis=-1, keepdims=True).astype(jnp.int32)
    slot_two = jnp.sum(before * two, axis=-1, keepdims=True).astype(jnp.int32)
    target = lax.broadcasted_iota(jnp.int32, lead_ref.shape, 1)
    lead = (target == routes_ref[:, 0:1] * SLOTS + slot_one).astype(F32).astype(BF16)
    follow = (target == routes_ref[:, 1:2] * SLOTS + slot_two).astype(F32).astype(BF16)
    lead_ref[...] = lead
    next_ref[...] = follow
    sent = lax.dot_general(lead + follow, hidden_ref[...], TN, preferred_element_type=F32)
    sent_ref[...] = sent.astype(BF16).reshape(sent_ref.shape)


def finish_attention(state, inside, decayed, stream, gain, routes, experts):
    length, width = stream.shape
    return pl.pallas_call(
        hidden_kernel,
        out_shape=(
            jax.ShapeDtypeStruct((length, width), BF16),
            jax.ShapeDtypeStruct((experts, SLOTS, width), BF16),
            jax.ShapeDtypeStruct((length, experts * SLOTS), BF16),
            jax.ShapeDtypeStruct((length, experts * SLOTS), BF16),
        ),
        in_specs=[whole()] * 6,
        out_specs=[whole()] * 4,
        compiler_params=params(56),
    )(state, inside, decayed, stream, gain, routes)


def norm_kernel(rows_ref, gain_ref, out_ref):
    parts, _, width = rows_ref.shape
    rows = [rows_ref[i].astype(F32) for i in range(parts)]
    squares = sum(jnp.sum(r * r, axis=-1, keepdims=True) for r in rows)
    scale = lax.rsqrt(squares / (parts * width) + STABILIZER)
    for i, r in enumerate(rows):
        part = slice(i * width, (i + 1) * width)
        out_ref[:, part] = (r * scale * gain_ref[:, part]).astype(BF16)


def norm_rows(rows, gain):
    return pl.pallas_call(
        norm_kernel,
        out_shape=jax.ShapeDtypeStruct((SLOTS, FEATURES), BF16),
        in_specs=[whole()] * 2,
        out_specs=whole(),
        compiler_params=params(16),
    )(rows, gain)


PACKED = 640
CHUNK = 1536
LIMIT = 24


def expert_kernel(groups, loads, *refs):
    x_refs, refs = refs[: 2 * groups], refs[2 * groups :]
    own_refs, other_refs, refs = refs[:3], refs[3:6], refs[6:]
    out_refs, refs = refs[: 2 * groups], refs[2 * groups :]
    copies = ()
    if loads:
        here_refs, refs, sems = refs[:3], refs[3:-1], refs[-1]
        copies = [
            pltpu.make_async_copy(other_refs[i], here_refs[i], sems.at[i]) for i in range(3)
        ]
        for copy in copies:
            copy.start()
        other_refs = here_refs
    sums = refs[0]
    hidden = own_refs[0].shape[0]
    for pair, weights in enumerate((own_refs[:2], other_refs[:2])):
        for w, ref in enumerate(weights):
            if pair and loads:
                copies[w].wait()
            for at in range(0, FEATURES, CHUNK):
                half, start = divmod(at, HALF)
                x = [x_ref[:, start : start + CHUNK] for x_ref in x_refs[half::2]]
                x = jnp.concatenate(x, axis=0)
                product = lax.dot_general(
                    ref[:, at : at + CHUNK], x, NT, preferred_element_type=F32
                )
                slot = 2 * pair + w
                sums[slot] = product if at == 0 else sums[slot] + product

    rows = groups * GROUP
    blank = PACKED - 2 * hidden
    activated = [silu(sums[2 * w]) * sums[2 * w + 1] for w in range(2)]
    activated.append(jnp.zeros((blank, rows), F32))
    activated = jnp.transpose(jnp.concatenate(activated, axis=0)).astype(BF16)

    if loads:
        copies[2].wait()
    for at in range(0, FEATURES, CHUNK):
        half, start = divmod(at, HALF)
        weights = [ref[:, at : at + CHUNK] for ref in (own_refs[2], other_refs[2])]
        weights = jnp.concatenate(weights + [jnp.zeros((blank, CHUNK), BF16)], axis=0)
        product = jnp.dot(activated, weights, preferred_element_type=F32).astype(BF16)
        for g in range(groups):
            out_refs[2 * g + half][:, start : start + CHUNK] = product[g * GROUP : (g + 1) * GROUP]


def expert(xs, own, other, loads=False):
    groups = len(xs) // 2
    hidden = own[0].shape[0]
    rows = groups * GROUP
    out_shape = (jax.ShapeDtypeStruct((GROUP, HALF), BF16),) * (2 * groups)
    scratch = [pltpu.VMEM((4, hidden, rows), F32)]
    if loads:
        out_shape += tuple(jax.ShapeDtypeStruct(w.shape, w.dtype) for w in other)
        scratch.append(pltpu.SemaphoreType.DMA((3,)))
    out = pl.pallas_call(
        lambda *refs: expert_kernel(groups, loads, *refs),
        out_shape=out_shape,
        in_specs=[whole()] * (2 * groups + 3) + [whole(pl.ANY if loads else pltpu.VMEM)] * 3,
        out_specs=(whole(),) * len(out_shape),
        scratch_shapes=scratch,
        compiler_params=params(LIMIT),
        cost_estimate=pl.CostEstimate(
            flops=2 * 256 * FEATURES * 6 * hidden,
            bytes_accessed=FEATURES * 6 * hidden * 2,
            transcendentals=0,
        ),
    )(*xs, *own, *other)
    return (out[: 2 * groups], out[2 * groups :]) if loads else out


def total_kernel(own_ref, *refs):
    out_ref = refs[-1]
    parts, _, width = out_ref.shape
    for i in range(parts):
        part = slice(i * width, (i + 1) * width)
        total = own_ref[0, :, part]
        for ref in refs[:-1]:
            total += ref[:, part].astype(F32)
        out_ref[i] = total.astype(BF16)


def total_rows(own, arrived, experts):
    return pl.pallas_call(
        total_kernel,
        grid=(1,),
        out_shape=jax.ShapeDtypeStruct((experts, SLOTS, FEATURES // experts), BF16),
        in_specs=[pl.BlockSpec((1, SLOTS, FEATURES), lambda i: (0, 0, 0))] + [whole()] * 3,
        out_specs=whole(),
        compiler_params=params(16),
    )(own, *arrived)


def mix_kernel(back_ref, lead_ref, next_ref, gates_ref, hidden_ref, out_ref):
    rows = back_ref[...].reshape(lead_ref.shape[1], out_ref.shape[1])
    one = jnp.dot(lead_ref[...], rows, preferred_element_type=F32)
    two = jnp.dot(next_ref[...], rows, preferred_element_type=F32)
    gates = gates_ref[...]
    moe = gates[:, 0:1] * one + gates[:, 1:2] * two
    out_ref[...] = (hidden_ref[...].astype(F32) + moe).astype(BF16)


def mix(back, lead, follow, gates, hidden):
    return pl.pallas_call(
        mix_kernel,
        out_shape=jax.ShapeDtypeStruct(hidden.shape, BF16),
        in_specs=[whole()] * 5,
        out_specs=whole(),
        compiler_params=params(16),
    )(back, lead, follow, gates, hidden)


FIRST, SECOND = 0, 1


def gather_first(block):
    after = send(block, FIRST, -1)
    before = send(block, FIRST, 1)
    opposite = send(block, FIRST, 2)
    blocks = (block, after, before, opposite)
    return tuple(
        jnp.concatenate([b[:, i * HALF : (i + 1) * HALF] for b in blocks], axis=0)
        for i in range(2)
    )


def added(*terms):
    return sum(t.astype(F32) for t in terms)


def body(
    query,
    keys,
    values,
    stream,
    log_decay,
    attn_gain,
    routes,
    gate_weights,
    moe_gain,
    w_gate,
    w_up,
    w_down,
):
    experts = w_gate.shape[0] * lax.axis_size("exp")
    blocks = lax.axis_size("ctx")
    gate, up, down = w_gate[0].T, w_up[0].T, w_down[0]
    sibling = chip_pairs(lambda core: (0, 0), 1)
    other_gate = lax.ppermute(gate, "ctx", sibling)
    other_up = lax.ppermute(up, "ctx", sibling)
    other_down = lax.ppermute(down, "ctx", sibling)

    pieces, inside, decayed = attend_locally(query, keys, values, log_decay.T, blocks)
    pieces = lax.all_to_all(pieces, "ctx", split_axis=0, concat_axis=0, tiled=True)
    place = lax.axis_index("ctx").astype(jnp.int32).reshape(1)
    states = scan_states(place, pieces)
    states = lax.all_to_all(states, "ctx", split_axis=0, concat_axis=0, tiled=True)
    states, other_gate, other_up, other_down = lax.optimization_barrier(
        (states, other_gate, other_up, other_down)
    )
    hidden, sent, lead, follow = finish_attention(
        states, inside, decayed, stream, attn_gain.reshape(1, -1), routes, experts
    )
    arrived = lax.all_to_all(sent, "exp", split_axis=0, concat_axis=0, tiled=True)
    rows = norm_rows(arrived, moe_gain.reshape(1, -1))
    mine, other = (gate, up, down), (other_gate, other_up, other_down)

    own = gather_first(rows)
    after_one = send(own[0], SECOND, -1)
    before_two = send(own[1], SECOND, 1)
    after_two = send(own[1], SECOND, -1)
    before_one = send(own[0], SECOND, 1)
    opposite = (send(after_one, SECOND, -1), send(before_two, SECOND, 1))
    beside, other = expert((after_one, after_two, before_one, before_two), mine, other, True)
    opposite, beside = lax.optimization_barrier((opposite, beside))
    to_after_one, to_after_two, to_before_one, to_before_two = beside
    from_after_one = send(to_before_one, SECOND, -1)
    from_before_two = send(to_after_two, SECOND, 1)
    far = expert(opposite, mine, other)
    far_one, far_two = far
    through = (send(far_one, SECOND, 1), send(far_two, SECOND, -1))
    own, from_after_one, from_before_two = lax.optimization_barrier(
        (own, from_after_one, from_before_two)
    )
    here = expert(own, mine, other)
    through, here = lax.optimization_barrier((through, here))
    through_after, through_before = through
    here_one, here_two = here
    from_before_one = send(added(to_after_one, through_after).astype(BF16), SECOND, 1)
    from_after_two = send(added(to_before_two, through_before).astype(BF16), SECOND, -1)
    sums = jnp.concatenate(
        [
            added(here_one, from_after_one, from_before_one),
            added(here_two, from_after_two, from_before_two),
        ],
        axis=1,
    ).reshape(SIDE, SLOTS, FEATURES)
    rounded = sums.astype(BF16)
    from_before = send(rounded[1], FIRST, 1)
    from_after = send(rounded[2], FIRST, -1)
    from_opposite = send(rounded[3], FIRST, 2)
    summed = total_rows(sums, (from_before, from_after, from_opposite), experts)
    returned = lax.all_to_all(summed, "exp", split_axis=0, concat_axis=0, tiled=True)
    return mix(returned, lead, follow, gate_weights, hidden)


def solution(mesh):
    return jax.shard_map(
        body,
        mesh=mesh,
        in_specs=(
            P("ctx", "exp"),
            P("ctx", "exp"),
            P("ctx", "exp"),
            P("ctx", "exp"),
            P("ctx", "exp"),
            P("exp"),
            P("ctx", None),
            P("ctx", None),
            P(),
            P("exp", None, "ctx"),
            P("exp", None, "ctx"),
            P("exp", "ctx", None),
        ),
        out_specs=P("ctx", "exp"),
        check_vma=False,
    )
```

```python
import jax
import jax.numpy as jnp
from jax import lax
from jax.experimental import pallas as pl
from jax.experimental.pallas import tpu as pltpu
from jax.sharding import PartitionSpec as P

STABILIZER = 1e-05
HIGHEST = lax.Precision.HIGHEST
F32 = jnp.float32
BF16 = jnp.bfloat16
NT = (((1,), (1,)), ((), ()))
TN = (((0,), (0,)), ((), ()))
SIDE = 4
CORES = 2
SLOTS = 32
GROUP = SIDE * SLOTS
PIECE = 24
FEATURES = 6144
HALF = FEATURES // 2


def whole(memory=pltpu.VMEM):
    return pl.BlockSpec(memory_space=memory)


def params(mib):
    return pltpu.CompilerParams(vmem_limit_bytes=mib << 20)


def chip_pairs(step, flip=0):
    pairs = []
    for y in range(SIDE):
        for x in range(SIDE):
            for core in range(CORES):
                dy, dx = step(core)
                to = (y + dy) % SIDE * SIDE + (x + dx) % SIDE
                pairs.append(((y * SIDE + x) * CORES + core, to * CORES + (core + flip) % CORES))
    return pairs


def send(rows, axis, distance):
    along_x = ((0, distance), (distance, 0))
    return lax.ppermute(rows, "ctx", chip_pairs(lambda core: along_x[(core + axis) % CORES]))


def silu(v):
    return v / (1.0 + jnp.exp(-v))


def lower_triangle(length):
    row = lax.broadcasted_iota(jnp.int32, (length, length), 0)
    col = lax.broadcasted_iota(jnp.int32, (length, length), 1)
    return row >= col


def widened(rate_ref, wide):
    wide[...] = jnp.zeros_like(wide)
    wide[: rate_ref.shape[0]] = rate_ref[...]
    return wide[...]


def summary_kernel(k_ref, v_ref, rate_ref, piece_ref, wide):
    length, width = k_ref.shape
    heads = rate_ref.shape[0]
    head = width // heads
    lower = lower_triangle(length).astype(F32)
    cumulated = lax.dot_general(
        lower, widened(rate_ref, wide), NT, precision=HIGHEST, preferred_element_type=F32
    )
    total = cumulated[length - 1 : length, :]
    tails = jnp.exp(cumulated - total)
    states = []
    for h in range(heads):
        part = slice(h * head, (h + 1) * head)
        ka = silu(k_ref[:, part].astype(F32)) * tails[:, h : h + 1]
        states.append(
            lax.dot_general(ka.astype(BF16), v_ref[:, part], TN, preferred_element_type=F32)
        )
    first = total.astype(BF16).astype(F32)
    second = (total - first).astype(BF16).astype(F32)
    third = total - first - second
    line = lax.broadcasted_iota(jnp.int32, (8, total.shape[1]), 0)
    notes = jnp.where(line == 0, first, jnp.where(line == 1, second, jnp.where(line == 2, third, 0.0)))
    count = piece_ref.shape[0]
    state = jnp.concatenate(states, axis=0).reshape(count, PIECE, head)
    notes = jnp.broadcast_to(notes[None], (count,) + notes.shape)
    piece_ref[...] = jnp.concatenate([state, notes], axis=1).astype(BF16)


def summarize(keys, values, rates, count):
    return pl.pallas_call(
        summary_kernel,
        out_shape=jax.ShapeDtypeStruct((count, PIECE + 8, 128), BF16),
        in_specs=[whole()] * 3,
        out_specs=whole(),
        scratch_shapes=[pltpu.VMEM((128, keys.shape[0]), F32)],
        compiler_params=params(56),
    )(keys, values, rates)


def local_kernel(q_ref, k_ref, v_ref, rate_ref, routes_ref, inside_ref, decayed_ref, lead_ref, next_ref, wide):
    length, width = q_ref.shape
    heads = rate_ref.shape[0]
    head = width // heads
    causal = lower_triangle(length)
    lower = causal.astype(F32)
    rates = widened(rate_ref, wide)
    cumulated = lax.dot_general(lower, rates, NT, precision=HIGHEST, preferred_element_type=F32)
    across = lax.dot_general(
        rates[:8], lower, NT, precision=HIGHEST, preferred_element_type=F32
    )
    for h in range(heads):
        part = slice(h * head, (h + 1) * head)
        qa = silu(q_ref[:, part].astype(F32))
        ka = silu(k_ref[:, part].astype(F32))
        down = cumulated[:, h : h + 1]
        spread = jnp.where(causal, down - across[h : h + 1, :], 0.0)
        weights = jnp.where(causal, jnp.exp(-spread), 0.0)
        scores = lax.dot_general(qa.astype(BF16), ka.astype(BF16), NT, preferred_element_type=F32)
        inside_ref[:, part] = jnp.dot(
            (scores * weights).astype(BF16), v_ref[:, part], preferred_element_type=F32
        )
        decayed_ref[:, part] = (qa * jnp.exp(-down)).astype(BF16)

    lane = lax.broadcasted_iota(jnp.int32, (length, 128), 1)
    one = (lane == routes_ref[:, 0:1]).astype(F32)
    two = (lane == routes_ref[:, 1:2]).astype(F32)
    row = lax.broadcasted_iota(jnp.int32, (length, length), 0)
    col = lax.broadcasted_iota(jnp.int32, (length, length), 1)
    earlier = (row > col).astype(BF16)
    before = jnp.dot(earlier, (one + two).astype(BF16), preferred_element_type=F32)
    slot_one = jnp.sum(before * one, axis=-1, keepdims=True).astype(jnp.int32)
    slot_two = jnp.sum(before * two, axis=-1, keepdims=True).astype(jnp.int32)
    target = lax.broadcasted_iota(jnp.int32, lead_ref.shape, 1)
    lead = target == routes_ref[:, 0:1] * SLOTS + slot_one
    follow = target == routes_ref[:, 1:2] * SLOTS + slot_two
    lead_ref[...] = lead.astype(F32).astype(BF16)
    next_ref[...] = follow.astype(F32).astype(BF16)


def attend_locally(query, keys, values, rates, routes, experts):
    length, width = query.shape
    return pl.pallas_call(
        local_kernel,
        out_shape=(
            jax.ShapeDtypeStruct((length, width), F32),
            jax.ShapeDtypeStruct((length, width), BF16),
            jax.ShapeDtypeStruct((length, experts * SLOTS), BF16),
            jax.ShapeDtypeStruct((length, experts * SLOTS), BF16),
        ),
        in_specs=[whole()] * 5,
        out_specs=[whole()] * 4,
        scratch_shapes=[pltpu.VMEM((128, length), F32)],
        compiler_params=params(56),
        cost_estimate=pl.CostEstimate(
            flops=2 * 6 * 2 * length * length * width, bytes_accessed=2 << 20, transcendentals=0
        ),
    )(query, keys, values, rates, routes)


def scan_kernel(place_ref, pieces_ref, out_ref):
    count, rows, lanes = pieces_ref.shape
    pieces = pieces_ref[...].astype(F32)
    notes = pieces[:, PIECE:]
    total = notes[:, 0:1] + notes[:, 1:2] + notes[:, 2:3]
    row = lax.broadcasted_iota(jnp.int32, (PIECE, lanes), 0) + place_ref[0] * PIECE
    own = lax.shift_right_logical(row, 7) == lax.broadcasted_iota(jnp.int32, (PIECE, lanes), 1)
    decay = jnp.sum(jnp.where(own[None], jnp.exp(-total), 0.0), axis=-1, keepdims=True)
    state = jnp.zeros((PIECE, lanes), F32)
    blank = jnp.zeros((rows - PIECE, lanes), F32)
    for i in range(count):
        out_ref[i] = jnp.concatenate([state, blank], axis=0).astype(BF16)
        state = decay[i] * state + pieces[i, :PIECE]


def scan_states(place, pieces):
    return pl.pallas_call(
        scan_kernel,
        out_shape=jax.ShapeDtypeStruct(pieces.shape, BF16),
        in_specs=[whole(pltpu.SMEM), whole()],
        out_specs=whole(),
        compiler_params=params(56),
    )(place, pieces)


def hidden_kernel(
    state_ref, inside_ref, decayed_ref, stream_ref, gain_ref, lead_ref, next_ref, hidden_ref, sent_ref
):
    width = stream_ref.shape[1]
    head = 128
    state = state_ref[...].astype(F32)[:, :PIECE].reshape(width, head).astype(BF16)
    placing = lead_ref[...] + next_ref[...]
    parts, rows, _ = sent_ref.shape
    for h in range(width // head):
        part = slice(h * head, (h + 1) * head)
        carried = jnp.dot(decayed_ref[:, part], state[part], preferred_element_type=F32)
        attended = inside_ref[:, part] + carried
        scale = lax.rsqrt(jnp.mean(attended * attended, axis=-1, keepdims=True) + STABILIZER)
        hidden = stream_ref[:, part].astype(F32) + attended * scale * gain_ref[:, part]
        hidden = hidden.astype(BF16)
        hidden_ref[:, part] = hidden
        sent = lax.dot_general(placing, hidden, TN, preferred_element_type=F32)
        sent_ref[:, :, part] = sent.astype(BF16).reshape(parts, rows, head)


def finish_attention(state, inside, decayed, stream, gain, lead, follow, experts):
    length, width = stream.shape
    return pl.pallas_call(
        hidden_kernel,
        out_shape=(
            jax.ShapeDtypeStruct((length, width), BF16),
            jax.ShapeDtypeStruct((experts, SLOTS, width), BF16),
        ),
        in_specs=[whole()] * 7,
        out_specs=[whole()] * 2,
        compiler_params=params(56),
    )(state, inside, decayed, stream, gain, lead, follow)


def norm_kernel(rows_ref, gain_ref, out_ref):
    parts, _, width = rows_ref.shape
    rows = [rows_ref[i].astype(F32) for i in range(parts)]
    squares = sum(jnp.sum(r * r, axis=-1, keepdims=True) for r in rows)
    scale = lax.rsqrt(squares / (parts * width) + STABILIZER)
    for i, r in enumerate(rows):
        part = slice(i * width, (i + 1) * width)
        out_ref[:, part] = (r * scale * gain_ref[:, part]).astype(BF16)


def norm_rows(rows, gain):
    return pl.pallas_call(
        norm_kernel,
        out_shape=jax.ShapeDtypeStruct((SLOTS, FEATURES), BF16),
        in_specs=[whole()] * 2,
        out_specs=whole(),
        compiler_params=params(16),
    )(rows, gain)


PACKED = 640
CHUNK = 1536
LIMIT = 24


def load_kernel(*refs):
    count = len(refs) // 2
    sems = refs[-1]
    copies = [pltpu.make_async_copy(refs[i], refs[count + i], sems.at[i]) for i in range(count)]
    for copy in copies:
        copy.start()
    for copy in copies:
        copy.wait()


def load(weights):
    count = len(weights)
    return pl.pallas_call(
        load_kernel,
        out_shape=tuple(jax.ShapeDtypeStruct(w.shape, w.dtype) for w in weights),
        in_specs=[whole(pl.ANY)] * count,
        out_specs=(whole(),) * count,
        scratch_shapes=[pltpu.SemaphoreType.DMA((count,))],
        compiler_params=params(16),
        cost_estimate=pl.CostEstimate(
            flops=0, bytes_accessed=2 * sum(w.size for w in weights), transcendentals=0
        ),
    )(*weights)


def expert_kernel(layout, count, *refs):
    x_refs, refs = refs[:count], refs[count:]
    weights, refs = refs[:6], refs[6:]
    out_refs, sums = refs[:-1], refs[-1]
    groups = len(layout)
    own_refs, other_refs = weights[:3], weights[3:]
    hidden = own_refs[0].shape[0]
    for slot, ref in enumerate(own_refs[:2] + other_refs[:2]):
        for at in range(0, FEATURES, CHUNK):
            half, start = divmod(at, HALF)
            x = []
            for group in layout:
                for piece in group:
                    index, offset = piece[half]
                    x.append(x_refs[index][:, offset + start : offset + start + CHUNK])
            x = jnp.concatenate(x, axis=0)
            product = lax.dot_general(ref[:, at : at + CHUNK], x, NT, preferred_element_type=F32)
            sums[slot] = product if at == 0 else sums[slot] + product

    rows = groups * GROUP
    blank = PACKED - 2 * hidden
    activated = [silu(sums[2 * w]) * sums[2 * w + 1] for w in range(2)]
    activated.append(jnp.zeros((blank, rows), F32))
    activated = jnp.transpose(jnp.concatenate(activated, axis=0)).astype(BF16)

    for at in range(0, FEATURES, CHUNK):
        half, start = divmod(at, HALF)
        weights = [ref[:, at : at + CHUNK] for ref in (own_refs[2], other_refs[2])]
        weights = jnp.concatenate(weights + [jnp.zeros((blank, CHUNK), BF16)], axis=0)
        product = jnp.dot(activated, weights, preferred_element_type=F32).astype(BF16)
        for g in range(groups):
            out_refs[2 * g + half][:, start : start + CHUNK] = product[g * GROUP : (g + 1) * GROUP]


def expert(groups, own, other):
    xs, layout = [], []
    for group in groups:
        pieces = []
        for piece in group:
            if isinstance(piece, tuple):
                pieces.append(((len(xs), 0), (len(xs) + 1, 0)))
                xs += piece
            else:
                pieces.append(((len(xs), 0), (len(xs), HALF)))
                xs.append(piece)
        layout.append(pieces)
    hidden = own[0].shape[0]
    rows = len(groups) * GROUP
    outs = 2 * len(groups)
    return pl.pallas_call(
        lambda *refs: expert_kernel(layout, len(xs), *refs),
        out_shape=(jax.ShapeDtypeStruct((GROUP, HALF), BF16),) * outs,
        in_specs=[whole()] * (len(xs) + 6),
        out_specs=(whole(),) * outs,
        scratch_shapes=[pltpu.VMEM((4, hidden, rows), F32)],
        compiler_params=params(LIMIT),
        cost_estimate=pl.CostEstimate(
            flops=2 * 256 * FEATURES * 6 * hidden,
            bytes_accessed=FEATURES * 6 * hidden * 2,
            transcendentals=0,
        ),
    )(*xs, *own, *other)


def meet_kernel(here_one, here_two, a_one, a_two, b_one, b_two, own_ref, *out_refs):
    for i, refs in enumerate(((here_one, a_one, b_one), (here_two, a_two, b_two))):
        part = slice(i * HALF, (i + 1) * HALF)
        for block in range(SIDE):
            rows = slice(block * SLOTS, (block + 1) * SLOTS)
            total = sum(ref[rows].astype(F32) for ref in refs)
            if block == 0:
                own_ref[:, part] = total
            else:
                out_refs[block - 1][:, part] = total.astype(BF16)


def meet(*terms):
    block = jax.ShapeDtypeStruct((SLOTS, FEATURES), BF16)
    return pl.pallas_call(
        meet_kernel,
        out_shape=(jax.ShapeDtypeStruct((SLOTS, FEATURES), F32), block, block, block),
        in_specs=[whole()] * 6,
        out_specs=(whole(),) * 4,
        compiler_params=params(16),
    )(*terms)


def total_kernel(own_ref, *refs):
    out_ref = refs[-1]
    parts, _, width = out_ref.shape
    for i in range(parts):
        part = slice(i * width, (i + 1) * width)
        total = own_ref[:, part]
        for ref in refs[:-1]:
            total += ref[:, part].astype(F32)
        out_ref[i] = total.astype(BF16)


def total_rows(own, arrived, experts):
    return pl.pallas_call(
        total_kernel,
        out_shape=jax.ShapeDtypeStruct((experts, SLOTS, FEATURES // experts), BF16),
        in_specs=[whole()] * 4,
        out_specs=whole(),
        compiler_params=params(16),
    )(own, *arrived)


def mix_kernel(back_ref, lead_ref, next_ref, gates_ref, hidden_ref, out_ref):
    rows = back_ref[...].reshape(lead_ref.shape[1], out_ref.shape[1])
    one = jnp.dot(lead_ref[...], rows, preferred_element_type=F32)
    two = jnp.dot(next_ref[...], rows, preferred_element_type=F32)
    gates = gates_ref[...]
    moe = gates[:, 0:1] * one + gates[:, 1:2] * two
    out_ref[...] = (hidden_ref[...].astype(F32) + moe).astype(BF16)


def mix(back, lead, follow, gates, hidden):
    return pl.pallas_call(
        mix_kernel,
        out_shape=jax.ShapeDtypeStruct(hidden.shape, BF16),
        in_specs=[whole()] * 5,
        out_specs=whole(),
        compiler_params=params(16),
    )(back, lead, follow, gates, hidden)


FIRST, SECOND = 0, 1


def neighbours(block, axis):
    return send(block, axis, -1), send(block, axis, 1)


def relayed(after, before, axis):
    return send(after[:, :HALF], axis, -1), send(before[:, HALF:], axis, 1)


def added(*terms):
    return sum(t.astype(F32) for t in terms)


def body(
    query,
    keys,
    values,
    stream,
    log_decay,
    attn_gain,
    routes,
    gate_weights,
    moe_gain,
    w_gate,
    w_up,
    w_down,
):
    experts = w_gate.shape[0] * lax.axis_size("exp")
    blocks = lax.axis_size("ctx")
    gate, up, down = w_gate[0].T, w_up[0].T, w_down[0]
    sibling = chip_pairs(lambda core: (0, 0), 1)
    other_gate = lax.ppermute(gate, "ctx", sibling)
    other_up = lax.ppermute(up, "ctx", sibling)
    other_down = lax.ppermute(down, "ctx", sibling)

    rates = log_decay.T
    pieces = summarize(keys, values, rates, blocks)
    pieces = lax.all_to_all(pieces, "ctx", split_axis=0, concat_axis=0, tiled=True)
    place = lax.axis_index("ctx").astype(jnp.int32).reshape(1)
    states = scan_states(place, pieces)
    states = lax.all_to_all(states, "ctx", split_axis=0, concat_axis=0, tiled=True)
    states, other_gate, other_up, other_down = lax.optimization_barrier(
        (states, other_gate, other_up, other_down)
    )
    inside, decayed, lead, follow = attend_locally(query, keys, values, rates, routes, experts)
    hidden, sent = finish_attention(
        states, inside, decayed, stream, attn_gain.reshape(1, -1), lead, follow, experts
    )
    arrived = lax.all_to_all(sent, "exp", split_axis=0, concat_axis=0, tiled=True)
    rows = norm_rows(arrived, moe_gain.reshape(1, -1))
    mine, other = (gate, up, down), (other_gate, other_up, other_down)

    rows, other = lax.optimization_barrier((rows, other))
    after, before = neighbours(rows, FIRST)
    after, before, other = lax.optimization_barrier((after, before, load(other)))
    near = jnp.concatenate([rows, after, before], axis=0)
    opposite = jnp.concatenate(relayed(after, before, FIRST), axis=1)
    near_after, near_before = neighbours(near, SECOND)
    last_after, last_before = neighbours(opposite, SECOND)
    near_far = relayed(near_after, near_before, SECOND)
    last_far = relayed(last_after, last_before, SECOND)
    beside = expert(
        ((near_after, last_after), (near_before, last_before)), mine, other
    )
    near_far, last_far, beside = lax.optimization_barrier((near_far, last_far, beside))
    to_after_one, to_after_two, to_before_one, to_before_two = beside
    from_after_one = send(to_before_one, SECOND, -1)
    from_before_two = send(to_after_two, SECOND, 1)
    far_one, far_two = expert(((near_far, last_far),), mine, other)
    through = (send(far_one, SECOND, 1), send(far_two, SECOND, -1))
    near, from_after_one, from_before_two = lax.optimization_barrier(
        (near, from_after_one, from_before_two)
    )
    here = expert(((near, opposite),), mine, other)
    through, here = lax.optimization_barrier((through, here))
    through_after, through_before = through
    here_one, here_two = here
    from_before_one = send(added(to_after_one, through_after).astype(BF16), SECOND, 1)
    from_after_two = send(added(to_before_two, through_before).astype(BF16), SECOND, -1)
    kept, to_after, to_before, to_opposite = meet(
        here_one, here_two, from_after_one, from_after_two, from_before_one, from_before_two
    )
    from_opposite = send(to_opposite, FIRST, 2)
    from_before = send(to_after, FIRST, 1)
    from_after = send(to_before, FIRST, -1)
    summed = total_rows(kept, (from_before, from_after, from_opposite), experts)
    returned = lax.all_to_all(summed, "exp", split_axis=0, concat_axis=0, tiled=True)
    return mix(returned, lead, follow, gate_weights, hidden)


def solution(mesh):
    return jax.shard_map(
        body,
        mesh=mesh,
        in_specs=(
            P("ctx", "exp"),
            P("ctx", "exp"),
            P("ctx", "exp"),
            P("ctx", "exp"),
            P("ctx", "exp"),
            P("exp"),
            P("ctx", None),
            P("ctx", None),
            P(),
            P("exp", None, "ctx"),
            P("exp", None, "ctx"),
            P("exp", "ctx", None),
        ),
        out_specs=P("ctx", "exp"),
        check_vma=False,
    )
```

```python
import jax
import jax.numpy as jnp
from jax import lax
from jax.experimental import pallas as pl
from jax.experimental.pallas import tpu as pltpu
from jax.sharding import PartitionSpec as P

STABILIZER = 1e-05
HIGHEST = lax.Precision.HIGHEST
F32 = jnp.float32
BF16 = jnp.bfloat16
NT = (((1,), (1,)), ((), ()))
TN = (((0,), (0,)), ((), ()))
SIDE = 4
CORES = 2
SLOTS = 32
GROUP = SIDE * SLOTS
PIECE = 24
FEATURES = 6144
HALF = FEATURES // 2


def whole(memory=pltpu.VMEM):
    return pl.BlockSpec(memory_space=memory)


def params(mib):
    return pltpu.CompilerParams(vmem_limit_bytes=mib << 20)


def chip_pairs(step, flip=0):
    pairs = []
    for y in range(SIDE):
        for x in range(SIDE):
            for core in range(CORES):
                dy, dx = step(core)
                to = (y + dy) % SIDE * SIDE + (x + dx) % SIDE
                pairs.append(((y * SIDE + x) * CORES + core, to * CORES + (core + flip) % CORES))
    return pairs


def send(rows, axis, distance):
    along_x = ((0, distance), (distance, 0))
    return lax.ppermute(rows, "ctx", chip_pairs(lambda core: along_x[(core + axis) % CORES]))


def silu(v):
    return v / (1.0 + jnp.exp(-v))


def lower_triangle(length):
    row = lax.broadcasted_iota(jnp.int32, (length, length), 0)
    col = lax.broadcasted_iota(jnp.int32, (length, length), 1)
    return row >= col


def widened(rate_ref, wide):
    wide[...] = jnp.zeros_like(wide)
    wide[: rate_ref.shape[0]] = rate_ref[...]
    return wide[...]


def summary_kernel(k_ref, v_ref, rate_ref, piece_ref, wide):
    length, width = k_ref.shape
    heads = rate_ref.shape[0]
    head = width // heads
    lower = lower_triangle(length).astype(F32)
    cumulated = lax.dot_general(
        lower, widened(rate_ref, wide), NT, precision=HIGHEST, preferred_element_type=F32
    )
    total = cumulated[length - 1 : length, :]
    tails = jnp.exp(cumulated - total)
    states = []
    for h in range(heads):
        part = slice(h * head, (h + 1) * head)
        ka = silu(k_ref[:, part].astype(F32)) * tails[:, h : h + 1]
        states.append(
            lax.dot_general(ka.astype(BF16), v_ref[:, part], TN, preferred_element_type=F32)
        )
    first = total.astype(BF16).astype(F32)
    second = (total - first).astype(BF16).astype(F32)
    third = total - first - second
    line = lax.broadcasted_iota(jnp.int32, (8, total.shape[1]), 0)
    notes = jnp.where(line == 0, first, jnp.where(line == 1, second, jnp.where(line == 2, third, 0.0)))
    count = piece_ref.shape[0]
    state = jnp.concatenate(states, axis=0).reshape(count, PIECE, head)
    notes = jnp.broadcast_to(notes[None], (count,) + notes.shape)
    piece_ref[...] = jnp.concatenate([state, notes], axis=1).astype(BF16)


def summarize(keys, values, rates, count):
    return pl.pallas_call(
        summary_kernel,
        out_shape=jax.ShapeDtypeStruct((count, PIECE + 8, 128), BF16),
        in_specs=[whole()] * 3,
        out_specs=whole(),
        scratch_shapes=[pltpu.VMEM((128, keys.shape[0]), F32)],
        compiler_params=params(56),
    )(keys, values, rates)


def local_kernel(q_ref, k_ref, v_ref, rate_ref, routes_ref, inside_ref, decayed_ref, lead_ref, next_ref, wide):
    length, width = q_ref.shape
    heads = rate_ref.shape[0]
    head = width // heads
    causal = lower_triangle(length)
    lower = causal.astype(F32)
    rates = widened(rate_ref, wide)
    cumulated = lax.dot_general(lower, rates, NT, precision=HIGHEST, preferred_element_type=F32)
    across = lax.dot_general(
        rates[:8], lower, NT, precision=HIGHEST, preferred_element_type=F32
    )
    for h in range(heads):
        part = slice(h * head, (h + 1) * head)
        qa = silu(q_ref[:, part].astype(F32))
        ka = silu(k_ref[:, part].astype(F32))
        down = cumulated[:, h : h + 1]
        spread = jnp.where(causal, down - across[h : h + 1, :], 0.0)
        weights = jnp.where(causal, jnp.exp(-spread), 0.0)
        scores = lax.dot_general(qa.astype(BF16), ka.astype(BF16), NT, preferred_element_type=F32)
        inside_ref[:, part] = jnp.dot(
            (scores * weights).astype(BF16), v_ref[:, part], preferred_element_type=F32
        )
        decayed_ref[:, part] = (qa * jnp.exp(-down)).astype(BF16)

    lane = lax.broadcasted_iota(jnp.int32, (length, 128), 1)
    one = (lane == routes_ref[:, 0:1]).astype(F32)
    two = (lane == routes_ref[:, 1:2]).astype(F32)
    row = lax.broadcasted_iota(jnp.int32, (length, length), 0)
    col = lax.broadcasted_iota(jnp.int32, (length, length), 1)
    earlier = (row > col).astype(BF16)
    before = jnp.dot(earlier, (one + two).astype(BF16), preferred_element_type=F32)
    slot_one = jnp.sum(before * one, axis=-1, keepdims=True).astype(jnp.int32)
    slot_two = jnp.sum(before * two, axis=-1, keepdims=True).astype(jnp.int32)
    target = lax.broadcasted_iota(jnp.int32, lead_ref.shape, 1)
    lead = target == routes_ref[:, 0:1] * SLOTS + slot_one
    follow = target == routes_ref[:, 1:2] * SLOTS + slot_two
    lead_ref[...] = lead.astype(F32).astype(BF16)
    next_ref[...] = follow.astype(F32).astype(BF16)


def attend_locally(query, keys, values, rates, routes, experts):
    length, width = query.shape
    return pl.pallas_call(
        local_kernel,
        out_shape=(
            jax.ShapeDtypeStruct((length, width), F32),
            jax.ShapeDtypeStruct((length, width), BF16),
            jax.ShapeDtypeStruct((length, experts * SLOTS), BF16),
            jax.ShapeDtypeStruct((length, experts * SLOTS), BF16),
        ),
        in_specs=[whole()] * 5,
        out_specs=[whole()] * 4,
        scratch_shapes=[pltpu.VMEM((128, length), F32)],
        compiler_params=params(56),
        cost_estimate=pl.CostEstimate(
            flops=2 * 6 * 2 * length * length * width, bytes_accessed=2 << 20, transcendentals=0
        ),
    )(query, keys, values, rates, routes)


def scan_kernel(place_ref, pieces_ref, out_ref):
    count, rows, lanes = pieces_ref.shape
    pieces = pieces_ref[...].astype(F32)
    notes = pieces[:, PIECE:]
    total = notes[:, 0:1] + notes[:, 1:2] + notes[:, 2:3]
    row = lax.broadcasted_iota(jnp.int32, (PIECE, lanes), 0) + place_ref[0] * PIECE
    own = lax.shift_right_logical(row, 7) == lax.broadcasted_iota(jnp.int32, (PIECE, lanes), 1)
    decay = jnp.sum(jnp.where(own[None], jnp.exp(-total), 0.0), axis=-1, keepdims=True)
    state = jnp.zeros((PIECE, lanes), F32)
    blank = jnp.zeros((rows - PIECE, lanes), F32)
    for i in range(count):
        out_ref[i] = jnp.concatenate([state, blank], axis=0).astype(BF16)
        state = decay[i] * state + pieces[i, :PIECE]


def scan_states(place, pieces):
    return pl.pallas_call(
        scan_kernel,
        out_shape=jax.ShapeDtypeStruct(pieces.shape, BF16),
        in_specs=[whole(pltpu.SMEM), whole()],
        out_specs=whole(),
        compiler_params=params(56),
    )(place, pieces)


def hidden_kernel(
    state_ref, inside_ref, decayed_ref, stream_ref, gain_ref, lead_ref, next_ref, hidden_ref, sent_ref
):
    width = stream_ref.shape[1]
    head = 128
    state = state_ref[...].astype(F32)[:, :PIECE].reshape(width, head).astype(BF16)
    placing = lead_ref[...] + next_ref[...]
    parts, rows, _ = sent_ref.shape
    for h in range(width // head):
        part = slice(h * head, (h + 1) * head)
        carried = jnp.dot(decayed_ref[:, part], state[part], preferred_element_type=F32)
        attended = inside_ref[:, part] + carried
        scale = lax.rsqrt(jnp.mean(attended * attended, axis=-1, keepdims=True) + STABILIZER)
        hidden = stream_ref[:, part].astype(F32) + attended * scale * gain_ref[:, part]
        hidden = hidden.astype(BF16)
        hidden_ref[:, part] = hidden
        sent = lax.dot_general(placing, hidden, TN, preferred_element_type=F32)
        sent_ref[:, :, part] = sent.astype(BF16).reshape(parts, rows, head)


def finish_attention(state, inside, decayed, stream, gain, lead, follow, experts):
    length, width = stream.shape
    return pl.pallas_call(
        hidden_kernel,
        out_shape=(
            jax.ShapeDtypeStruct((length, width), BF16),
            jax.ShapeDtypeStruct((experts, SLOTS, width), BF16),
        ),
        in_specs=[whole()] * 7,
        out_specs=[whole()] * 2,
        compiler_params=params(56),
    )(state, inside, decayed, stream, gain, lead, follow)


def norm_kernel(rows_ref, gain_ref, out_ref):
    parts, _, width = rows_ref.shape
    rows = [rows_ref[i].astype(F32) for i in range(parts)]
    squares = sum(jnp.sum(r * r, axis=-1, keepdims=True) for r in rows)
    scale = lax.rsqrt(squares / (parts * width) + STABILIZER)
    for i, r in enumerate(rows):
        part = slice(i * width, (i + 1) * width)
        out_ref[:, part] = (r * scale * gain_ref[:, part]).astype(BF16)


def norm_rows(rows, gain):
    return pl.pallas_call(
        norm_kernel,
        out_shape=jax.ShapeDtypeStruct((SLOTS, FEATURES), BF16),
        in_specs=[whole()] * 2,
        out_specs=whole(),
        compiler_params=params(16),
    )(rows, gain)


PACKED = 640
CHUNK = 1536
LIMIT = 24


def load_kernel(*refs):
    count = len(refs) // 2
    sems = refs[-1]
    copies = [pltpu.make_async_copy(refs[i], refs[count + i], sems.at[i]) for i in range(count)]
    for copy in copies:
        copy.start()
    for copy in copies:
        copy.wait()


def load(weights):
    count = len(weights)
    return pl.pallas_call(
        load_kernel,
        out_shape=tuple(jax.ShapeDtypeStruct(w.shape, w.dtype) for w in weights),
        in_specs=[whole(pl.ANY)] * count,
        out_specs=(whole(),) * count,
        scratch_shapes=[pltpu.SemaphoreType.DMA((count,))],
        compiler_params=params(16),
        cost_estimate=pl.CostEstimate(
            flops=0, bytes_accessed=2 * sum(w.size for w in weights), transcendentals=0
        ),
    )(*weights)


def expert_kernel(layout, count, *refs):
    x_refs, refs = refs[:count], refs[count:]
    weights, refs = refs[:6], refs[6:]
    out_refs, sums = refs[:-1], refs[-1]
    groups = len(layout)
    own_refs, other_refs = weights[:3], weights[3:]
    hidden = own_refs[0].shape[0]
    for slot, ref in enumerate(own_refs[:2] + other_refs[:2]):
        for at in range(0, FEATURES, CHUNK):
            half, start = divmod(at, HALF)
            x = []
            for group in layout:
                for piece in group:
                    index, offset = piece[half]
                    x.append(x_refs[index][:, offset + start : offset + start + CHUNK])
            x = jnp.concatenate(x, axis=0)
            product = lax.dot_general(ref[:, at : at + CHUNK], x, NT, preferred_element_type=F32)
            sums[slot] = product if at == 0 else sums[slot] + product

    rows = groups * GROUP
    blank = PACKED - 2 * hidden
    activated = [silu(sums[2 * w]) * sums[2 * w + 1] for w in range(2)]
    activated.append(jnp.zeros((blank, rows), F32))
    activated = jnp.transpose(jnp.concatenate(activated, axis=0)).astype(BF16)

    for at in range(0, FEATURES, CHUNK):
        half, start = divmod(at, HALF)
        weights = [ref[:, at : at + CHUNK] for ref in (own_refs[2], other_refs[2])]
        weights = jnp.concatenate(weights + [jnp.zeros((blank, CHUNK), BF16)], axis=0)
        product = jnp.dot(activated, weights, preferred_element_type=F32).astype(BF16)
        for g in range(groups):
            out_refs[2 * g + half][:, start : start + CHUNK] = product[g * GROUP : (g + 1) * GROUP]


def expert(groups, own, other):
    xs, layout = [], []
    for group in groups:
        pieces = []
        for piece in group:
            if isinstance(piece, tuple):
                pieces.append(((len(xs), 0), (len(xs) + 1, 0)))
                xs += piece
            else:
                pieces.append(((len(xs), 0), (len(xs), HALF)))
                xs.append(piece)
        layout.append(pieces)
    hidden = own[0].shape[0]
    rows = len(groups) * GROUP
    outs = 2 * len(groups)
    return pl.pallas_call(
        lambda *refs: expert_kernel(layout, len(xs), *refs),
        out_shape=(jax.ShapeDtypeStruct((GROUP, HALF), BF16),) * outs,
        in_specs=[whole()] * (len(xs) + 6),
        out_specs=(whole(),) * outs,
        scratch_shapes=[pltpu.VMEM((4, hidden, rows), F32)],
        compiler_params=params(LIMIT),
        cost_estimate=pl.CostEstimate(
            flops=2 * 256 * FEATURES * 6 * hidden,
            bytes_accessed=FEATURES * 6 * hidden * 2,
            transcendentals=0,
        ),
    )(*xs, *own, *other)


def meet_kernel(here_one, here_two, a_one, a_two, b_one, b_two, own_ref, *out_refs):
    for i, refs in enumerate(((here_one, a_one, b_one), (here_two, a_two, b_two))):
        part = slice(i * HALF, (i + 1) * HALF)
        for block in range(SIDE):
            rows = slice(block * SLOTS, (block + 1) * SLOTS)
            total = sum(ref[rows].astype(F32) for ref in refs)
            if block == 0:
                own_ref[:, part] = total
            else:
                out_refs[block - 1][:, part] = total.astype(BF16)


def meet(*terms):
    block = jax.ShapeDtypeStruct((SLOTS, FEATURES), BF16)
    return pl.pallas_call(
        meet_kernel,
        out_shape=(jax.ShapeDtypeStruct((SLOTS, FEATURES), F32), block, block, block),
        in_specs=[whole()] * 6,
        out_specs=(whole(),) * 4,
        compiler_params=params(16),
    )(*terms)


def total_kernel(own_ref, *refs):
    out_ref = refs[-1]
    parts, _, width = out_ref.shape
    for i in range(parts):
        part = slice(i * width, (i + 1) * width)
        total = own_ref[:, part]
        for ref in refs[:-1]:
            total += ref[:, part].astype(F32)
        out_ref[i] = total.astype(BF16)


def total_rows(own, arrived, experts):
    return pl.pallas_call(
        total_kernel,
        out_shape=jax.ShapeDtypeStruct((experts, SLOTS, FEATURES // experts), BF16),
        in_specs=[whole()] * 4,
        out_specs=whole(),
        compiler_params=params(16),
    )(own, *arrived)


def mix_kernel(back_ref, lead_ref, next_ref, gates_ref, hidden_ref, out_ref):
    rows = back_ref[...].reshape(lead_ref.shape[1], out_ref.shape[1])
    one = jnp.dot(lead_ref[...], rows, preferred_element_type=F32)
    two = jnp.dot(next_ref[...], rows, preferred_element_type=F32)
    gates = gates_ref[...]
    moe = gates[:, 0:1] * one + gates[:, 1:2] * two
    out_ref[...] = (hidden_ref[...].astype(F32) + moe).astype(BF16)


def mix(back, lead, follow, gates, hidden):
    return pl.pallas_call(
        mix_kernel,
        out_shape=jax.ShapeDtypeStruct(hidden.shape, BF16),
        in_specs=[whole()] * 5,
        out_specs=whole(),
        compiler_params=params(16),
    )(back, lead, follow, gates, hidden)


FIRST, SECOND = 0, 1


def neighbours(block, axis):
    return send(block, axis, -1), send(block, axis, 1)


def relayed(after, before, axis):
    return send(after[:, :HALF], axis, -1), send(before[:, HALF:], axis, 1)


def added(*terms):
    return sum(t.astype(F32) for t in terms)


def body(
    query,
    keys,
    values,
    stream,
    log_decay,
    attn_gain,
    routes,
    gate_weights,
    moe_gain,
    w_gate,
    w_up,
    w_down,
):
    experts = w_gate.shape[0] * lax.axis_size("exp")
    blocks = lax.axis_size("ctx")
    gate, up, down = w_gate[0].T, w_up[0].T, w_down[0]
    sibling = chip_pairs(lambda core: (0, 0), 1)
    other_gate = lax.ppermute(gate, "ctx", sibling)
    other_up = lax.ppermute(up, "ctx", sibling)
    other_down = lax.ppermute(down, "ctx", sibling)

    rates = log_decay.T
    pieces = summarize(keys, values, rates, blocks)
    pieces = lax.all_to_all(pieces, "ctx", split_axis=0, concat_axis=0, tiled=True)
    place = lax.axis_index("ctx").astype(jnp.int32).reshape(1)
    states = scan_states(place, pieces)
    states = lax.all_to_all(states, "ctx", split_axis=0, concat_axis=0, tiled=True)
    states, other_gate, other_up, other_down = lax.optimization_barrier(
        (states, other_gate, other_up, other_down)
    )
    inside, decayed, lead, follow = attend_locally(query, keys, values, rates, routes, experts)
    hidden, sent = finish_attention(
        states, inside, decayed, stream, attn_gain.reshape(1, -1), lead, follow, experts
    )
    arrived = lax.all_to_all(sent, "exp", split_axis=0, concat_axis=0, tiled=True)
    rows = norm_rows(arrived, moe_gain.reshape(1, -1))
    mine, other = (gate, up, down), (other_gate, other_up, other_down)

    rows, other = lax.optimization_barrier((rows, other))
    after, before = neighbours(rows, FIRST)
    after, before, other = lax.optimization_barrier((after, before, load(other)))
    near = jnp.concatenate([rows, after, before], axis=0)
    opposite = jnp.concatenate(relayed(after, before, FIRST), axis=1)
    near_after, near_before = neighbours(near, SECOND)
    last_after, last_before = neighbours(opposite, SECOND)
    near_far = relayed(near_after, near_before, SECOND)
    last_far = relayed(last_after, last_before, SECOND)
    beside = expert(
        ((near_after, last_after), (near_before, last_before)), mine, other
    )
    near_far, last_far, beside = lax.optimization_barrier((near_far, last_far, beside))
    to_after_one, to_after_two, to_before_one, to_before_two = beside
    far = expert(((near_far, last_far),), mine, other)
    far, near, to_before_one, to_after_two = lax.optimization_barrier(
        (far, near, to_before_one, to_after_two)
    )
    far_one, far_two = far
    through = (send(far_one, SECOND, 1), send(far_two, SECOND, -1))
    from_after_one = send(to_before_one, SECOND, -1)
    from_before_two = send(to_after_two, SECOND, 1)
    here = expert(((near, opposite),), mine, other)
    through, here = lax.optimization_barrier((through, here))
    through_after, through_before = through
    here_one, here_two = here
    from_before_one = send(added(to_after_one, through_after).astype(BF16), SECOND, 1)
    from_after_two = send(added(to_before_two, through_before).astype(BF16), SECOND, -1)
    kept, to_after, to_before, to_opposite = meet(
        here_one, here_two, from_after_one, from_after_two, from_before_one, from_before_two
    )
    from_opposite = send(to_opposite, FIRST, 2)
    from_before = send(to_after, FIRST, 1)
    from_after = send(to_before, FIRST, -1)
    summed = total_rows(kept, (from_before, from_after, from_opposite), experts)
    returned = lax.all_to_all(summed, "exp", split_axis=0, concat_axis=0, tiled=True)
    return mix(returned, lead, follow, gate_weights, hidden)


def solution(mesh):
    return jax.shard_map(
        body,
        mesh=mesh,
        in_specs=(
            P("ctx", "exp"),
            P("ctx", "exp"),
            P("ctx", "exp"),
            P("ctx", "exp"),
            P("ctx", "exp"),
            P("exp"),
            P("ctx", None),
            P("ctx", None),
            P(),
            P("exp", None, "ctx"),
            P("exp", None, "ctx"),
            P("exp", "ctx", None),
        ),
        out_specs=P("ctx", "exp"),
        check_vma=False,
    )
```

```python
import jax
import jax.numpy as jnp
from jax import lax
from jax.experimental import pallas as pl
from jax.experimental.pallas import tpu as pltpu
from jax.sharding import PartitionSpec as P

STABILIZER = 1e-05
HIGHEST = lax.Precision.HIGHEST
F32 = jnp.float32
BF16 = jnp.bfloat16
NT = (((1,), (1,)), ((), ()))
TN = (((0,), (0,)), ((), ()))
SIDE = 4
CORES = 2
SLOTS = 32
GROUP = SIDE * SLOTS
PIECE = 24
FEATURES = 6144
HALF = FEATURES // 2


def whole(memory=pltpu.VMEM):
    return pl.BlockSpec(memory_space=memory)


def params(mib):
    return pltpu.CompilerParams(vmem_limit_bytes=mib << 20)


def chip_pairs(step, flip=0):
    pairs = []
    for y in range(SIDE):
        for x in range(SIDE):
            for core in range(CORES):
                dy, dx = step(core)
                to = (y + dy) % SIDE * SIDE + (x + dx) % SIDE
                pairs.append(((y * SIDE + x) * CORES + core, to * CORES + (core + flip) % CORES))
    return pairs


def send(rows, axis, distance):
    along_x = ((0, distance), (distance, 0))
    return lax.ppermute(rows, "ctx", chip_pairs(lambda core: along_x[(core + axis) % CORES]))


def silu(v):
    return v / (1.0 + jnp.exp(-v))


def lower_triangle(length):
    row = lax.broadcasted_iota(jnp.int32, (length, length), 0)
    col = lax.broadcasted_iota(jnp.int32, (length, length), 1)
    return row >= col


def widened(rate_ref, wide):
    wide[...] = jnp.zeros_like(wide)
    wide[: rate_ref.shape[0]] = rate_ref[...]
    return wide[...]


def summary_kernel(k_ref, v_ref, rate_ref, piece_ref, wide):
    length, width = k_ref.shape
    heads = rate_ref.shape[0]
    head = width // heads
    lower = lower_triangle(length).astype(F32)
    cumulated = lax.dot_general(
        lower, widened(rate_ref, wide), NT, precision=HIGHEST, preferred_element_type=F32
    )
    total = cumulated[length - 1 : length, :]
    tails = jnp.exp(cumulated - total)
    states = []
    for h in range(heads):
        part = slice(h * head, (h + 1) * head)
        ka = silu(k_ref[:, part].astype(F32)) * tails[:, h : h + 1]
        states.append(
            lax.dot_general(ka.astype(BF16), v_ref[:, part], TN, preferred_element_type=F32)
        )
    first = total.astype(BF16).astype(F32)
    second = (total - first).astype(BF16).astype(F32)
    third = total - first - second
    line = lax.broadcasted_iota(jnp.int32, (8, total.shape[1]), 0)
    notes = jnp.where(line == 0, first, jnp.where(line == 1, second, jnp.where(line == 2, third, 0.0)))
    count = piece_ref.shape[0]
    state = jnp.concatenate(states, axis=0).reshape(count, PIECE, head)
    notes = jnp.broadcast_to(notes[None], (count,) + notes.shape)
    piece_ref[...] = jnp.concatenate([state, notes], axis=1).astype(BF16)


def summarize(keys, values, rates, count):
    return pl.pallas_call(
        summary_kernel,
        out_shape=jax.ShapeDtypeStruct((count, PIECE + 8, 128), BF16),
        in_specs=[whole()] * 3,
        out_specs=whole(),
        scratch_shapes=[pltpu.VMEM((128, keys.shape[0]), F32)],
        compiler_params=params(56),
    )(keys, values, rates)


def local_kernel(q_ref, k_ref, v_ref, rate_ref, routes_ref, inside_ref, decayed_ref, lead_ref, next_ref, wide):
    length, width = q_ref.shape
    heads = rate_ref.shape[0]
    head = width // heads
    causal = lower_triangle(length)
    lower = causal.astype(F32)
    rates = widened(rate_ref, wide)
    cumulated = lax.dot_general(lower, rates, NT, precision=HIGHEST, preferred_element_type=F32)
    across = lax.dot_general(
        rates[:8], lower, NT, precision=HIGHEST, preferred_element_type=F32
    )
    for h in range(heads):
        part = slice(h * head, (h + 1) * head)
        qa = silu(q_ref[:, part].astype(F32))
        ka = silu(k_ref[:, part].astype(F32))
        down = cumulated[:, h : h + 1]
        spread = jnp.where(causal, down - across[h : h + 1, :], 0.0)
        weights = jnp.where(causal, jnp.exp(-spread), 0.0)
        scores = lax.dot_general(qa.astype(BF16), ka.astype(BF16), NT, preferred_element_type=F32)
        inside_ref[:, part] = jnp.dot(
            (scores * weights).astype(BF16), v_ref[:, part], preferred_element_type=F32
        )
        decayed_ref[:, part] = (qa * jnp.exp(-down)).astype(BF16)

    lane = lax.broadcasted_iota(jnp.int32, (length, 128), 1)
    one = (lane == routes_ref[:, 0:1]).astype(F32)
    two = (lane == routes_ref[:, 1:2]).astype(F32)
    row = lax.broadcasted_iota(jnp.int32, (length, length), 0)
    col = lax.broadcasted_iota(jnp.int32, (length, length), 1)
    earlier = (row > col).astype(BF16)
    before = jnp.dot(earlier, (one + two).astype(BF16), preferred_element_type=F32)
    slot_one = jnp.sum(before * one, axis=-1, keepdims=True).astype(jnp.int32)
    slot_two = jnp.sum(before * two, axis=-1, keepdims=True).astype(jnp.int32)
    target = lax.broadcasted_iota(jnp.int32, lead_ref.shape, 1)
    lead = target == routes_ref[:, 0:1] * SLOTS + slot_one
    follow = target == routes_ref[:, 1:2] * SLOTS + slot_two
    lead_ref[...] = lead.astype(F32).astype(BF16)
    next_ref[...] = follow.astype(F32).astype(BF16)


def attend_locally(query, keys, values, rates, routes, experts):
    length, width = query.shape
    return pl.pallas_call(
        local_kernel,
        out_shape=(
            jax.ShapeDtypeStruct((length, width), F32),
            jax.ShapeDtypeStruct((length, width), BF16),
            jax.ShapeDtypeStruct((length, experts * SLOTS), BF16),
            jax.ShapeDtypeStruct((length, experts * SLOTS), BF16),
        ),
        in_specs=[whole()] * 5,
        out_specs=[whole()] * 4,
        scratch_shapes=[pltpu.VMEM((128, length), F32)],
        compiler_params=params(56),
        cost_estimate=pl.CostEstimate(
            flops=2 * 6 * 2 * length * length * width, bytes_accessed=2 << 20, transcendentals=0
        ),
    )(query, keys, values, rates, routes)


def scan_kernel(place_ref, pieces_ref, out_ref):
    count, rows, lanes = pieces_ref.shape
    pieces = pieces_ref[...].astype(F32)
    notes = pieces[:, PIECE:]
    total = notes[:, 0:1] + notes[:, 1:2] + notes[:, 2:3]
    row = lax.broadcasted_iota(jnp.int32, (PIECE, lanes), 0) + place_ref[0] * PIECE
    own = lax.shift_right_logical(row, 7) == lax.broadcasted_iota(jnp.int32, (PIECE, lanes), 1)
    decay = jnp.sum(jnp.where(own[None], jnp.exp(-total), 0.0), axis=-1, keepdims=True)
    state = jnp.zeros((PIECE, lanes), F32)
    blank = jnp.zeros((rows - PIECE, lanes), F32)
    for i in range(count):
        out_ref[i] = jnp.concatenate([state, blank], axis=0).astype(BF16)
        state = decay[i] * state + pieces[i, :PIECE]


def scan_states(place, pieces):
    return pl.pallas_call(
        scan_kernel,
        out_shape=jax.ShapeDtypeStruct(pieces.shape, BF16),
        in_specs=[whole(pltpu.SMEM), whole()],
        out_specs=whole(),
        compiler_params=params(56),
    )(place, pieces)


def hidden_kernel(
    state_ref, inside_ref, decayed_ref, stream_ref, gain_ref, lead_ref, next_ref, hidden_ref, sent_ref
):
    width = stream_ref.shape[1]
    head = 128
    state = state_ref[...].astype(F32)[:, :PIECE].reshape(width, head).astype(BF16)
    placing = lead_ref[...] + next_ref[...]
    parts, rows, _ = sent_ref.shape
    for h in range(width // head):
        part = slice(h * head, (h + 1) * head)
        carried = jnp.dot(decayed_ref[:, part], state[part], preferred_element_type=F32)
        attended = inside_ref[:, part] + carried
        scale = lax.rsqrt(jnp.mean(attended * attended, axis=-1, keepdims=True) + STABILIZER)
        hidden = stream_ref[:, part].astype(F32) + attended * scale * gain_ref[:, part]
        hidden = hidden.astype(BF16)
        hidden_ref[:, part] = hidden
        sent = lax.dot_general(placing, hidden, TN, preferred_element_type=F32)
        sent_ref[:, :, part] = sent.astype(BF16).reshape(parts, rows, head)


def finish_attention(state, inside, decayed, stream, gain, lead, follow, experts):
    length, width = stream.shape
    return pl.pallas_call(
        hidden_kernel,
        out_shape=(
            jax.ShapeDtypeStruct((length, width), BF16),
            jax.ShapeDtypeStruct((experts, SLOTS, width), BF16),
        ),
        in_specs=[whole()] * 7,
        out_specs=[whole()] * 2,
        compiler_params=params(56),
    )(state, inside, decayed, stream, gain, lead, follow)


def norm_kernel(rows_ref, far_gain_ref, out_ref, gain_ref, sem):
    fetch = pltpu.make_async_copy(far_gain_ref, gain_ref, sem)
    fetch.start()
    parts, _, width = rows_ref.shape
    rows = [rows_ref[i].astype(F32) for i in range(parts)]
    squares = sum(jnp.sum(r * r, axis=-1, keepdims=True) for r in rows)
    scale = lax.rsqrt(squares / (parts * width) + STABILIZER)
    fetch.wait()
    for i, r in enumerate(rows):
        part = slice(i * width, (i + 1) * width)
        out_ref[:, part] = (r * scale * gain_ref[:, part]).astype(BF16)


def norm_rows(rows, gain):
    return pl.pallas_call(
        norm_kernel,
        out_shape=jax.ShapeDtypeStruct((SLOTS, FEATURES), BF16),
        in_specs=[whole(), whole(pl.ANY)],
        out_specs=whole(),
        scratch_shapes=[pltpu.VMEM((1, FEATURES), F32), pltpu.SemaphoreType.DMA],
        compiler_params=params(16),
    )(rows, gain)


PACKED = 640
CHUNK = 1536
LIMIT = 24


def load_kernel(*refs):
    count = len(refs) // 2
    sems = refs[-1]
    copies = [pltpu.make_async_copy(refs[i], refs[count + i], sems.at[i]) for i in range(count)]
    for copy in copies:
        copy.start()
    for copy in copies:
        copy.wait()


def load(weights):
    count = len(weights)
    return pl.pallas_call(
        load_kernel,
        out_shape=tuple(jax.ShapeDtypeStruct(w.shape, w.dtype) for w in weights),
        in_specs=[whole(pl.ANY)] * count,
        out_specs=(whole(),) * count,
        scratch_shapes=[pltpu.SemaphoreType.DMA((count,))],
        compiler_params=params(16),
        cost_estimate=pl.CostEstimate(
            flops=0, bytes_accessed=2 * sum(w.size for w in weights), transcendentals=0
        ),
    )(*weights)


def expert_kernel(layout, count, *refs):
    x_refs, refs = refs[:count], refs[count:]
    weights, refs = refs[:6], refs[6:]
    out_refs, sums = refs[:-1], refs[-1]
    groups = len(layout)
    own_refs, other_refs = weights[:3], weights[3:]
    hidden = own_refs[0].shape[0]
    for slot, ref in enumerate(own_refs[:2] + other_refs[:2]):
        for at in range(0, FEATURES, CHUNK):
            half, start = divmod(at, HALF)
            x = []
            for group in layout:
                for piece in group:
                    index, offset = piece[half]
                    x.append(x_refs[index][:, offset + start : offset + start + CHUNK])
            x = jnp.concatenate(x, axis=0)
            product = lax.dot_general(ref[:, at : at + CHUNK], x, NT, preferred_element_type=F32)
            sums[slot] = product if at == 0 else sums[slot] + product

    rows = groups * GROUP
    blank = PACKED - 2 * hidden
    activated = [silu(sums[2 * w]) * sums[2 * w + 1] for w in range(2)]
    activated.append(jnp.zeros((blank, rows), F32))
    activated = jnp.transpose(jnp.concatenate(activated, axis=0)).astype(BF16)

    for at in range(0, FEATURES, CHUNK):
        half, start = divmod(at, HALF)
        weights = [ref[:, at : at + CHUNK] for ref in (own_refs[2], other_refs[2])]
        weights = jnp.concatenate(weights + [jnp.zeros((blank, CHUNK), BF16)], axis=0)
        product = jnp.dot(activated, weights, preferred_element_type=F32).astype(BF16)
        for g in range(groups):
            out_refs[2 * g + half][:, start : start + CHUNK] = product[g * GROUP : (g + 1) * GROUP]


def expert(groups, own, other):
    xs, layout = [], []
    for group in groups:
        pieces = []
        for piece in group:
            if isinstance(piece, tuple):
                pieces.append(((len(xs), 0), (len(xs) + 1, 0)))
                xs += piece
            else:
                pieces.append(((len(xs), 0), (len(xs), HALF)))
                xs.append(piece)
        layout.append(pieces)
    hidden = own[0].shape[0]
    rows = len(groups) * GROUP
    outs = 2 * len(groups)
    return pl.pallas_call(
        lambda *refs: expert_kernel(layout, len(xs), *refs),
        out_shape=(jax.ShapeDtypeStruct((GROUP, HALF), BF16),) * outs,
        in_specs=[whole()] * (len(xs) + 6),
        out_specs=(whole(),) * outs,
        scratch_shapes=[pltpu.VMEM((4, hidden, rows), F32)],
        compiler_params=params(LIMIT),
        cost_estimate=pl.CostEstimate(
            flops=2 * 256 * FEATURES * 6 * hidden,
            bytes_accessed=FEATURES * 6 * hidden * 2,
            transcendentals=0,
        ),
    )(*xs, *own, *other)


def meet_kernel(here_one, here_two, a_one, a_two, b_one, b_two, own_ref, *out_refs):
    for i, refs in enumerate(((here_one, a_one, b_one), (here_two, a_two, b_two))):
        part = slice(i * HALF, (i + 1) * HALF)
        for block in range(SIDE):
            rows = slice(block * SLOTS, (block + 1) * SLOTS)
            total = sum(ref[rows].astype(F32) for ref in refs)
            if block == 0:
                own_ref[:, part] = total
            else:
                out_refs[block - 1][:, part] = total.astype(BF16)


def meet(*terms):
    block = jax.ShapeDtypeStruct((SLOTS, FEATURES), BF16)
    return pl.pallas_call(
        meet_kernel,
        out_shape=(jax.ShapeDtypeStruct((SLOTS, FEATURES), F32), block, block, block),
        in_specs=[whole()] * 6,
        out_specs=(whole(),) * 4,
        compiler_params=params(16),
    )(*terms)


def total_kernel(own_ref, *refs):
    out_ref = refs[-1]
    parts, _, width = out_ref.shape
    for i in range(parts):
        part = slice(i * width, (i + 1) * width)
        total = own_ref[:, part]
        for ref in refs[:-1]:
            total += ref[:, part].astype(F32)
        out_ref[i] = total.astype(BF16)


def total_rows(own, arrived, experts):
    return pl.pallas_call(
        total_kernel,
        out_shape=jax.ShapeDtypeStruct((experts, SLOTS, FEATURES // experts), BF16),
        in_specs=[whole()] * 4,
        out_specs=whole(),
        compiler_params=params(16),
    )(own, *arrived)


def mix_kernel(back_ref, lead_ref, next_ref, gates_ref, hidden_ref, out_ref):
    rows = back_ref[...].reshape(lead_ref.shape[1], out_ref.shape[1])
    one = jnp.dot(lead_ref[...], rows, preferred_element_type=F32)
    two = jnp.dot(next_ref[...], rows, preferred_element_type=F32)
    gates = gates_ref[...]
    moe = gates[:, 0:1] * one + gates[:, 1:2] * two
    out_ref[...] = (hidden_ref[...].astype(F32) + moe).astype(BF16)


def mix(back, lead, follow, gates, hidden):
    return pl.pallas_call(
        mix_kernel,
        out_shape=jax.ShapeDtypeStruct(hidden.shape, BF16),
        in_specs=[whole()] * 5,
        out_specs=whole(),
        compiler_params=params(16),
    )(back, lead, follow, gates, hidden)


FIRST, SECOND = 0, 1


def neighbours(block, axis):
    return send(block, axis, -1), send(block, axis, 1)


def relayed(after, before, axis):
    return send(after[:, :HALF], axis, -1), send(before[:, HALF:], axis, 1)


def added(*terms):
    return sum(t.astype(F32) for t in terms)


def body(
    query,
    keys,
    values,
    stream,
    log_decay,
    attn_gain,
    routes,
    gate_weights,
    moe_gain,
    w_gate,
    w_up,
    w_down,
):
    experts = w_gate.shape[0] * lax.axis_size("exp")
    blocks = lax.axis_size("ctx")
    gate, up, down = w_gate[0].T, w_up[0].T, w_down[0]
    sibling = chip_pairs(lambda core: (0, 0), 1)
    other_gate = lax.ppermute(gate, "ctx", sibling)
    other_up = lax.ppermute(up, "ctx", sibling)
    other_down = lax.ppermute(down, "ctx", sibling)

    rates = log_decay.T
    pieces = summarize(keys, values, rates, blocks)
    pieces = lax.all_to_all(pieces, "ctx", split_axis=0, concat_axis=0, tiled=True)
    place = lax.axis_index("ctx").astype(jnp.int32).reshape(1)
    states = scan_states(place, pieces)
    states = lax.all_to_all(states, "ctx", split_axis=0, concat_axis=0, tiled=True)
    states, other_gate, other_up, other_down = lax.optimization_barrier(
        (states, other_gate, other_up, other_down)
    )
    inside, decayed, lead, follow = attend_locally(query, keys, values, rates, routes, experts)
    hidden, sent = finish_attention(
        states, inside, decayed, stream, attn_gain.reshape(1, -1), lead, follow, experts
    )
    arrived = lax.all_to_all(sent, "exp", split_axis=0, concat_axis=0, tiled=True)
    rows = norm_rows(arrived, moe_gain.reshape(1, -1))
    mine, other = (gate, up, down), (other_gate, other_up, other_down)

    rows, other = lax.optimization_barrier((rows, other))
    after, before = neighbours(rows, FIRST)
    after, before, other = lax.optimization_barrier((after, before, load(other)))
    near = jnp.concatenate([rows, after, before], axis=0)
    opposite = jnp.concatenate(relayed(after, before, FIRST), axis=1)
    near_after, near_before = neighbours(near, SECOND)
    last_after, last_before = neighbours(opposite, SECOND)
    near_far = relayed(near_after, near_before, SECOND)
    last_far = relayed(last_after, last_before, SECOND)
    beside = expert(
        ((near_after, last_after), (near_before, last_before)), mine, other
    )
    near_far, last_far, beside = lax.optimization_barrier((near_far, last_far, beside))
    to_after_one, to_after_two, to_before_one, to_before_two = beside
    far = expert(((near_far, last_far),), mine, other)
    far, near, to_before_one, to_after_two = lax.optimization_barrier(
        (far, near, to_before_one, to_after_two)
    )
    far_one, far_two = far
    through = (send(far_one, SECOND, 1), send(far_two, SECOND, -1))
    from_after_one = send(to_before_one, SECOND, -1)
    from_before_two = send(to_after_two, SECOND, 1)
    here = expert(((near, opposite),), mine, other)
    through, here = lax.optimization_barrier((through, here))
    through_after, through_before = through
    here_one, here_two = here
    from_before_one = send(added(to_after_one, through_after).astype(BF16), SECOND, 1)
    from_after_two = send(added(to_before_two, through_before).astype(BF16), SECOND, -1)
    kept, to_after, to_before, to_opposite = meet(
        here_one, here_two, from_after_one, from_after_two, from_before_one, from_before_two
    )
    from_opposite = send(to_opposite, FIRST, 2)
    from_before = send(to_after, FIRST, 1)
    from_after = send(to_before, FIRST, -1)
    summed = total_rows(kept, (from_before, from_after, from_opposite), experts)
    returned = lax.all_to_all(summed, "exp", split_axis=0, concat_axis=0, tiled=True)
    return mix(returned, lead, follow, gate_weights, hidden)


def solution(mesh):
    return jax.shard_map(
        body,
        mesh=mesh,
        in_specs=(
            P("ctx", "exp"),
            P("ctx", "exp"),
            P("ctx", "exp"),
            P("ctx", "exp"),
            P("ctx", "exp"),
            P("exp"),
            P("ctx", None),
            P("ctx", None),
            P(),
            P("exp", None, "ctx"),
            P("exp", None, "ctx"),
            P("exp", "ctx", None),
        ),
        out_specs=P("ctx", "exp"),
        check_vma=False,
    )
```
